512 devices in a mesh: band: 16 (over y_hi, z), dom: 32 (over y_lo, x, core).
Axes of the slice: x: 4, y: 8 (y_hi: 2, y_lo: 4; y = y_hi * 4 + y_lo), z: 8, core: 2. Of those that a mesh axis runs over, the one named last changes fastest.
Arguments:
- orbitals: float32 [64, 192, 48, 128], P('band', 'dom'), may hold values from -6 to 6
- occupation: float32 [64], P('band'), may hold values from 0.005 to 0.03
- dielectric: float32 [192, 48, 128], P('dom'), may hold values from 1 to 10
- core_density: float32 [192, 48, 128], P('dom'), may hold values from 0.05 to 0.5
- start_field: float32 [192, 48, 128], P('dom'), may hold values from -6 to 6
Outputs:
- potential: float32 [192, 48, 128], P('dom')
- filtered: float32 [64, 192, 48, 128], P('band', 'dom')
The draws below stay inside these ranges and needn't reach their ends.
All inputs are finite; a program needn't handle non-finite values.
Results may differ from the reference program's by a relative error of at most 0.00002.
Values sent between devices are 32-bit elements; how exact they have to be, the bound alone decides.
No kernel may reach another device: no remote copies, remote signals or barrier semaphores. Data moves between devices by JAX's collectives and lax.ppermute only.
A program may use at most 64 MiB of HBM per device.

```python
import math
import jax
import jax.numpy as jnp
from jax import lax

NORB = 64
NY = 48
NZ = 128
ITERS = 4
DEGREE = 4
NX = 192


def level_of(rng, extent, cuts, smallest, largest):
    gain = 1.0
    for axis_at, parts in cuts:
        draws = jax.random.uniform(jax.random.fold_in(jax.random.fold_in(rng, 6), axis_at), (parts,), jnp.float32, smallest / len(cuts), largest / len(cuts))
        gain = gain * jnp.repeat(jnp.exp(draws), extent[axis_at] // parts).reshape((-1,) + (1,) * (len(extent) - 1 - axis_at))
    return gain


def centred(rng, dims, spread, limit, pieces=(), held_as=jnp.bfloat16):
    drawn = spread * jax.random.normal(rng, dims, jnp.float32)
    if pieces:
        drawn = drawn * level_of(rng, dims, pieces, -0.22, 0.18)
    return jnp.clip(drawn, -limit, limit).astype(held_as)


def setup_inputs(seed: int = 0) -> dict:
    key_list = jax.random.split(jax.random.key(seed), 6)
    return {
        "orbitals": centred(key_list[0], (NORB, NX, NY, NZ), 1.0, 6.0, ((0, 16), (1, 32)), jnp.float32),
        "occupation": jnp.clip(jnp.exp(math.log(0.03) - 1.7917595 * jax.random.uniform(key_list[1], (NORB,), jnp.float32) ** level_of(key_list[1], (NORB,), ((0, 16),), -0.2, 0.2)), 0.005, 0.03),
        "dielectric": jnp.clip(jnp.exp(math.log(10.0) - 2.3025851 * jax.random.uniform(key_list[2], (NX, NY, NZ), jnp.float32) ** level_of(key_list[2], (NX, NY, NZ), ((0, 32),), -0.2, 0.2)), 1.0, 10.0),
        "core_density": jnp.clip(jnp.exp(math.log(0.5) - 2.3025851 * jax.random.uniform(key_list[3], (NX, NY, NZ), jnp.float32) ** level_of(key_list[3], (NX, NY, NZ), ((0, 32),), -0.2, 0.2)), 0.05, 0.5),
        "start_field": centred(key_list[4], (NX, NY, NZ), 1.0, 6.0, ((0, 32),), jnp.float32),
    }


coeff_one = 1.5
coeff_two = -0.15
coeff_three = 1.0 / 90.0
coeff_zero = -49.0 / 18.0
center_value = 5.25
half_value = 4.75
slater = -0.98474502184269641


def laplace(padded):
    size_x = padded.shape[-3] - 6
    size_y = padded.shape[-2] - 6
    size_z = padded.shape[-1] - 6
    core = padded[..., 3:3 + size_x, 3:3 + size_y, 3:3 + size_z]
    total = 3.0 * coeff_zero * core
    for dist, weight in ((1, coeff_one), (2, coeff_two), (3, coeff_three)):
        along = padded[..., 3 + dist:3 + dist + size_x, 3:3 + size_y, 3:3 + size_z]
        along = along + padded[..., 3 - dist:3 - dist + size_x, 3:3 + size_y, 3:3 + size_z]
        along = along + padded[..., 3:3 + size_x, 3 + dist:3 + dist + size_y, 3:3 + size_z]
        along = along + padded[..., 3:3 + size_x, 3 - dist:3 - dist + size_y, 3:3 + size_z]
        along = along + padded[..., 3:3 + size_x, 3:3 + size_y, 3 + dist:3 + dist + size_z]
        along = along + padded[..., 3:3 + size_x, 3:3 + size_y, 3 - dist:3 - dist + size_z]
        total = total + weight * along
    return total


def face_weights(permit, padded):
    weights = (
        0.5 * (permit + padded[2:, 1:-1, 1:-1]),
        0.5 * (permit + padded[:-2, 1:-1, 1:-1]),
        0.5 * (permit + padded[1:-1, 2:, 1:-1]),
        0.5 * (permit + padded[1:-1, :-2, 1:-1]),
        0.5 * (permit + padded[1:-1, 1:-1, 2:]),
        0.5 * (permit + padded[1:-1, 1:-1, :-2]),
    )
    denominator = weights[0] + weights[1] + weights[2] + weights[3] + weights[4] + weights[5]
    return weights, denominator


def sweep(padded, weights, denominator, source):
    numerator = weights[0] * padded[2:, 1:-1, 1:-1] + weights[1] * padded[:-2, 1:-1, 1:-1]
    numerator = numerator + weights[2] * padded[1:-1, 2:, 1:-1] + weights[3] * padded[1:-1, :-2, 1:-1]
    numerator = numerator + weights[4] * padded[1:-1, 1:-1, 2:] + weights[5] * padded[1:-1, 1:-1, :-2]
    return (numerator + source) / denominator


def reference(orbitals, occupation, dielectric, core_density, start_field):
    density = jnp.sum(occupation[:, None, None, None] * orbitals * orbitals, axis=0)
    weights, denominator = face_weights(dielectric, jnp.pad(dielectric, 1))
    source = 4.0 * density
    field = start_field
    for turn_index in range(ITERS):
        field = sweep(jnp.pad(field, 1), weights, denominator, source)
    potential = field + slater * jnp.cbrt(density + core_density)

    def hamil(block):
        return -0.5 * laplace(jnp.pad(block, 3)) + potential * block

    def one_orbital(orbital):
        before = orbital
        current = (hamil(orbital) - center_value * orbital) / half_value
        for turn_index in range(DEGREE - 1):
            nextone = 2.0 * (hamil(current) - center_value * current) / half_value - before
            before = current
            current = nextone
        return current

    filtered = lax.map(one_orbital, orbitals)
    return potential, filtered
```

```python
import jax
import jax.numpy as jnp
from jax import lax
from jax.experimental import pallas as pl
from jax.experimental.pallas import tpu as pltpu
from jax.sharding import PartitionSpec as P

NB = 4
BX = 6
NY = 48
NZ = 128
ROWS = BX * NY
TOP = 8
PADY = NY + 2 * TOP

COEFFS = (1.5, -0.15, 1.0 / 90.0)
COEFF_ZERO = -49.0 / 18.0
CENTER = 5.25
HALF = 4.75
SLATER = -0.9847450218426964
SCALE = -0.5 / HALF

VMEM_LIMIT = 48 * 1024 * 1024
ANY = pl.BlockSpec(memory_space=pl.ANY)
VM = pl.BlockSpec(memory_space=pltpu.VMEM)
SM = pl.BlockSpec(memory_space=pltpu.SMEM)
MID = pl.ds(TOP, NY)


def call(kernel, outs, in_specs, out_specs, scratch, args, flops):
    return pl.pallas_call(
        kernel,
        out_shape=[jax.ShapeDtypeStruct(s, jnp.float32) for s in outs],
        in_specs=in_specs,
        out_specs=out_specs,
        scratch_shapes=scratch,
        compiler_params=pltpu.CompilerParams(vmem_limit_bytes=VMEM_LIMIT),
        cost_estimate=pl.CostEstimate(flops=flops, bytes_accessed=2_000_000, transcendentals=0),
    )(*args)


def pack_kernel(chunks, occ, orb, diel, core, field, parts, packed, u, dens, sems):
    size = ROWS // chunks
    load = pltpu.make_async_copy(orb, u, sems.at[0])
    load.start()
    out = [
        pltpu.make_async_copy(orb, packed.at[pl.ds(0, NB)], sems.at[1]),
        pltpu.make_async_copy(field, packed.at[NB], sems.at[2]),
        pltpu.make_async_copy(diel, packed.at[NB + 1], sems.at[3]),
        pltpu.make_async_copy(core, packed.at[NB + 2], sems.at[4]),
    ]
    for c in out:
        c.start()
    load.wait()

    def plane(p, _):
        total = occ[0] * u[0, p] * u[0, p]
        for o in range(1, NB):
            total = total + occ[o] * u[o, p] * u[o, p]
        dens[pl.ds(pl.multiple_of(p * NY, NY), NY), :] = total
        return 0

    lax.fori_loop(0, BX, plane, 0)
    for c in range(chunks):
        parts[c] = dens[pl.ds(c * size, size), :]
    for c in out:
        c.wait()


def pack(chunks, occ, orb, diel, core, field):
    def kernel(*refs):
        pack_kernel(chunks, *refs)

    return call(
        kernel,
        [(chunks, ROWS // chunks, NZ), (NB + 3, BX, NY, NZ)],
        [SM, ANY, ANY, ANY, ANY],
        [VM, ANY],
        [
            pltpu.VMEM((NB, BX, NY, NZ), jnp.float32),
            pltpu.VMEM((ROWS, NZ), jnp.float32),
            pltpu.SemaphoreType.DMA((5,)),
        ],
        (occ, orb, diel, core, field),
        500_000,
    )


def join_kernel(chunks, got, left, right, rho, to_right, to_left, sems):
    size = ROWS // chunks
    copies = []
    for at, (src, edge, dst) in enumerate(
        (
            (left, BX - 1, to_right),
            (right, 0, to_left),
        )
    ):
        for k in range(2):
            copies.append(
                pltpu.make_async_copy(
                    src.at[NB + k, edge],
                    dst.at[pl.ds(ROWS + k * NY, NY)],
                    sems.at[2 * at + k],
                )
            )
    for c in copies:
        c.start()
    for c in range(chunks):
        value = got[c]
        for dst in (rho, to_right, to_left):
            dst[pl.ds(c * size, size), :] = value
    for c in copies:
        c.wait()


def join(chunks, got, left, right):
    def kernel(*refs):
        join_kernel(chunks, *refs)

    return call(
        kernel,
        [(ROWS, NZ), (ROWS + 2 * NY, NZ), (ROWS + 2 * NY, NZ)],
        [VM, ANY, ANY],
        [VM, VM, VM],
        [pltpu.SemaphoreType.DMA((4,))],
        (got, left, right),
        100_000,
    )


def lane_shift(value, dist, lane):
    ahead = jnp.where(lane < NZ - dist, pltpu.roll(value, NZ - dist, 1), 0.0)
    behind = jnp.where(lane >= dist, pltpu.roll(value, dist, 1), 0.0)
    return ahead + behind


def stencil(src, o, p, lane, factor):
    mid = src[o, p, MID, :]
    total = None
    for dist, weight in zip((1, 2, 3), COEFFS):
        along = src[o, p + dist, MID, :] + src[o, p - dist, MID, :]
        along = along + (src[o, p, pl.ds(TOP + dist, NY), :] + src[o, p, pl.ds(TOP - dist, NY), :])
        along = along + lane_shift(mid, dist, lane)
        term = (factor * SCALE * weight) * along
        total = term if total is None else total + term
    return total, mid


def zero_rows(ref, lead):
    blank = jnp.zeros((TOP, NZ), jnp.float32)

    def one(i, _):
        at = []
        for size in reversed(lead):
            at.append(lax.rem(i, size))
            i = lax.div(i, size)
        at = tuple(reversed(at))
        ref[(*at, pl.ds(0, TOP), slice(None))] = blank
        ref[(*at, pl.ds(TOP + NY, TOP), slice(None))] = blank
        return 0

    count = 1
    for size in lead:
        count *= size
    lax.fori_loop(0, count, one, 0)


def first_kernel(
    edges, orb, diel, core, field, rho, left, right, rho_left, rho_right,
    potential, y1_out, y2_out, diag_out,
    u, y1, fa, fb, di, rh, co, wts, sems, big_sems, out_sems,
):
    E = 3 * BX + 2
    orb_copies = [
        pltpu.make_async_copy(left.at[pl.ds(0, NB)], u.at[:, pl.ds(0, BX), MID, :], big_sems.at[0]),
        pltpu.make_async_copy(orb, u.at[:, pl.ds(BX, BX), MID, :], big_sems.at[1]),
        pltpu.make_async_copy(right.at[pl.ds(0, NB)], u.at[:, pl.ds(2 * BX, BX), MID, :], big_sems.at[2]),
    ]
    moves = []
    for k, (dst, own) in enumerate(((fa, field), (di, diel))):
        moves += [
            (left.at[NB + k], dst.at[pl.ds(1, BX), MID, :]),
            (own, dst.at[pl.ds(1 + BX, BX), MID, :]),
            (right.at[NB + k], dst.at[pl.ds(1 + 2 * BX, BX), MID, :]),
            (rho_left.at[BX + k], dst.at[0, MID, :]),
            (rho_right.at[BX + k], dst.at[E - 1, MID, :]),
        ]
    moves += [
        (rho_left.at[pl.ds(0, BX)], rh.at[pl.ds(0, BX)]),
        (rho, rh.at[pl.ds(BX, BX)]),
        (rho_right.at[pl.ds(0, BX)], rh.at[pl.ds(2 * BX, BX)]),
        (left.at[NB + 2, pl.ds(BX - 3, 3)], co.at[pl.ds(0, 3)]),
        (core, co.at[pl.ds(3, BX)]),
        (right.at[NB + 2, pl.ds(0, 3)], co.at[pl.ds(3 + BX, 3)]),
    ]
    copies = [pltpu.make_async_copy(s, d, sems.at[i]) for i, (s, d) in enumerate(moves)]
    for c in copies + orb_copies:
        c.start()
    has_left = edges[0] > 0
    has_right = edges[1] > 0
    zero_rows(fa, (E,))
    zero_rows(fb, (E,))
    zero_rows(di, (E,))
    zero_rows(u, (NB, 3 * BX))
    zero_rows(y1, (NB, 2 * BX))
    lane = lax.broadcasted_iota(jnp.int32, (NY, NZ), 1)
    for c in copies:
        c.wait()

    def inside(e):
        return ((e >= 1 + BX) | has_left) & ((e < 1 + 2 * BX) | has_right)

    def weigh(e, _):
        d = di[e, MID, :]
        xp = 0.5 * (d + di[e + 1, MID, :])
        xm = 0.5 * (d + di[e - 1, MID, :])
        yp = 0.5 * (d + di[e, pl.ds(TOP + 1, NY), :])
        ym = 0.5 * (d + di[e, pl.ds(TOP - 1, NY), :])
        last = lane == NZ - 1
        begin = lane == 0
        zp = 0.5 * (d + jnp.where(last, 0.0, pltpu.roll(d, NZ - 1, 1)))
        zm = 0.5 * (d + jnp.where(begin, 0.0, pltpu.roll(d, 1, 1)))
        den = xp + xm + yp + ym + zp + zm
        inverse = jnp.where(inside(e), 1.0 / den, 0.0)
        wts[0, e] = xp * inverse
        wts[1, e] = xm * inverse
        wts[2, e] = yp * inverse
        wts[3, e] = ym * inverse
        wts[4, e] = jnp.where(last, 0.0, zp * inverse)
        wts[5, e] = jnp.where(begin, 0.0, zm * inverse)
        wts[6, e] = 4.0 * rh[e - 1] * inverse
        return 0

    lax.fori_loop(1, E - 1, weigh, 0)

    def swept(src, e):
        mid = src[e, MID, :]
        total = wts[0, e] * src[e + 1, MID, :] + wts[1, e] * src[e - 1, MID, :]
        total = total + (wts[2, e] * src[e, pl.ds(TOP + 1, NY), :] + wts[3, e] * src[e, pl.ds(TOP - 1, NY), :])
        total = total + (wts[4, e] * pltpu.roll(mid, NZ - 1, 1) + wts[5, e] * pltpu.roll(mid, 1, 1))
        return total + wts[6, e]

    def sweep(src, dst, margin):
        def body(e, _):
            dst[e, MID, :] = swept(src, e)
            return 0

        lax.fori_loop(margin, E - margin, body, 0)

    sweep(fa, fb, 1)
    sweep(fb, fa, 2)
    sweep(fa, fb, 3)

    def last_sweep(j, _):
        e = j + 4
        x = rh[e - 1] + co[j]
        x = jnp.where(inside(e), x, 1.0)
        root = jnp.exp(jnp.log(x) * (1.0 / 3.0))
        root = root - (root - x / (root * root)) * (1.0 / 3.0)
        value = swept(fb, e) + SLATER * root
        fa[e, MID, :] = value
        diag_out[j] = (value - CENTER) * (1.0 / HALF) + 3.0 * COEFF_ZERO * SCALE
        return 0

    lax.fori_loop(0, 2 * BX, last_sweep, 0)
    for p in range(BX):
        potential[p] = fa[p + 1 + BX, MID, :]
    for c in orb_copies:
        c.wait()

    def step_one(i, _):
        o = lax.div(i, 2 * BX)
        j = lax.rem(i, 2 * BX)
        rest, mid = stencil(u, o, j + 3, lane, 1.0)
        here = ((j >= 3) | has_left) & ((j < 3 + BX) | has_right)
        y1[o, j, MID, :] = jnp.where(here, diag_out[j] * mid + rest, 0.0)
        return 0

    lax.fori_loop(0, NB * 2 * BX, step_one, 0)
    save = pltpu.make_async_copy(y1.at[:, :, MID, :], y1_out, out_sems.at[0])
    save.start()

    def step_two(i, _):
        o = lax.div(i, BX)
        j = lax.rem(i, BX)
        rest, mid = stencil(y1, o, j + 3, lane, 2.0)
        y2_out[o, j] = 2.0 * diag_out[j + 3] * mid + rest - u[o, j + BX, MID, :]
        return 0

    lax.fori_loop(0, NB * BX, step_two, 0)
    save.wait()


def first(edges, orb, diel, core, field, rho, left, right, rho_left, rho_right):
    E = 3 * BX + 2
    f = jnp.float32
    return call(
        first_kernel,
        [(BX, NY, NZ), (NB, 2 * BX, NY, NZ), (NB, BX, NY, NZ), (2 * BX, NY, NZ)],
        [SM] + [ANY] * 9,
        [VM, ANY, VM, VM],
        [
            pltpu.VMEM((NB, 3 * BX, PADY, NZ), f),
            pltpu.VMEM((NB, 2 * BX, PADY, NZ), f),
            pltpu.VMEM((E, PADY, NZ), f),
            pltpu.VMEM((E, PADY, NZ), f),
            pltpu.VMEM((E, PADY, NZ), f),
            pltpu.VMEM((3 * BX, NY, NZ), f),
            pltpu.VMEM((2 * BX, NY, NZ), f),
            pltpu.VMEM((7, E, NY, NZ), f),
            pltpu.SemaphoreType.DMA((16,)),
            pltpu.SemaphoreType.DMA((3,)),
            pltpu.SemaphoreType.DMA((1,)),
        ],
        (edges, orb, diel, core, field, rho, left, right, rho_left, rho_right),
        20_000_000,
    )


def second_kernel(edges, y1, y2, left, right, diag, out, u, y3, y1_in, sems):
    copies = [
        pltpu.make_async_copy(left, u.at[:, pl.ds(0, BX), MID, :], sems.at[0]),
        pltpu.make_async_copy(y2, u.at[:, pl.ds(BX, BX), MID, :], sems.at[1]),
        pltpu.make_async_copy(right, u.at[:, pl.ds(2 * BX, BX), MID, :], sems.at[2]),
        pltpu.make_async_copy(y1, y1_in, sems.at[3]),
    ]
    for c in copies:
        c.start()
    has_left = edges[0] > 0
    has_right = edges[1] > 0
    zero_rows(u, (NB, 3 * BX))
    zero_rows(y3, (NB, 2 * BX))
    lane = lax.broadcasted_iota(jnp.int32, (NY, NZ), 1)
    for c in copies:
        c.wait()

    def step_three(i, _):
        o = lax.div(i, 2 * BX)
        j = lax.rem(i, 2 * BX)
        rest, mid = stencil(u, o, j + 3, lane, 2.0)
        here = ((j >= 3) | has_left) & ((j < 3 + BX) | has_right)
        y3[o, j, MID, :] = jnp.where(here, 2.0 * diag[j] * mid + rest - y1_in[o, j], 0.0)
        return 0

    lax.fori_loop(0, NB * 2 * BX, step_three, 0)

    def step_four(i, _):
        o = lax.div(i, BX)
        j = lax.rem(i, BX)
        rest, mid = stencil(y3, o, j + 3, lane, 2.0)
        out[o, j] = 2.0 * diag[j + 3] * mid + rest - u[o, j + BX, MID, :]
        return 0

    lax.fori_loop(0, NB * BX, step_four, 0)


def second(edges, y1, y2, left, right, diag):
    f = jnp.float32
    return call(
        second_kernel,
        [(NB, BX, NY, NZ)],
        [SM, ANY, ANY, ANY, ANY, VM],
        [VM],
        [
            pltpu.VMEM((NB, 3 * BX, PADY, NZ), f),
            pltpu.VMEM((NB, 2 * BX, PADY, NZ), f),
            pltpu.VMEM((NB, 2 * BX, NY, NZ), f),
            pltpu.SemaphoreType.DMA((4,)),
        ],
        (edges, y1, y2, left, right, diag),
        15_000_000,
    )[0]


def from_sides(to_right, to_left):
    n = lax.axis_size("dom")
    left = lax.ppermute(to_right, "dom", [(i, i + 1) for i in range(n - 1)])
    right = lax.ppermute(to_left, "dom", [(i + 1, i) for i in range(n - 1)])
    return left, right


def local(orbitals, occupation, dielectric, core_density, start_field):
    bands = lax.axis_size("band")
    dom = lax.axis_index("dom")
    far = bands // 2
    groups = [list(range(far)), list(range(far, bands))]
    edges = jnp.stack([(dom > 0).astype(jnp.int32), (dom < lax.axis_size("dom") - 1).astype(jnp.int32)])

    parts, packed = pack(far, occupation, orbitals, dielectric, core_density, start_field)
    parts = lax.all_to_all(parts, "band", 0, 0, axis_index_groups=groups)
    mine = jnp.sum(parts, axis=0)
    other = lax.ppermute(mine, "band", [(i, (i + far) % bands) for i in range(bands)])
    left, right = from_sides(packed, packed)
    mine = mine + other
    got = lax.all_to_all(
        jnp.broadcast_to(mine[None], (far, *mine.shape)), "band", 0, 0, axis_index_groups=groups
    )
    rho, to_right, to_left = join(far, got, left, right)
    rho_left, rho_right = from_sides(to_right, to_left)
    cells = (-1, NY, NZ)
    potential, y1, y2, diag = first(
        edges, orbitals, dielectric, core_density, start_field, rho.reshape(cells), left, right,
        rho_left.reshape(cells), rho_right.reshape(cells),
    )
    y2_left, y2_right = from_sides(y2, y2)
    return potential, second(edges, y1, y2, y2_left, y2_right, diag)


def solution(mesh):
    return jax.shard_map(
        local,
        mesh=mesh,
        in_specs=(
            P("band", "dom", None, None),
            P("band"),
            P("dom", None, None),
            P("dom", None, None),
            P("dom", None, None),
        ),
        out_specs=(P("dom", None, None), P("band", "dom", None, None)),
        check_vma=False,
    )
```

```python
import jax
import jax.numpy as jnp
from jax import lax
from jax.experimental import pallas as pl
from jax.experimental.pallas import tpu as pltpu
from jax.sharding import PartitionSpec as P

NB = 4
BX = 6
NY = 48
NZ = 128
ROWS = BX * NY
STRIPS = 8
NV = NY // STRIPS

COEFFS = (1.5, -0.15, 1.0 / 90.0)
COEFF_ZERO = -49.0 / 18.0
CENTER = 5.25
HALF = 4.75
SLATER = -0.9847450218426964
SCALE = -0.5 / HALF

VMEM_LIMIT = 12 * 1024 * 1024
VMEM_ALL = 63 * 1024 * 1024
ANY = pl.BlockSpec(memory_space=pl.ANY)
HBM = pl.BlockSpec(memory_space=pltpu.HBM)
BESIDE_FAR = 20_000_000
BESIDE_NEAR = 80_000_000
VM = pl.BlockSpec(memory_space=pltpu.VMEM)
SM = pl.BlockSpec(memory_space=pltpu.SMEM)


def call(kernel, outs, in_specs, out_specs, scratch, args, moved=2_000_000, vmem=VMEM_LIMIT):
    return pl.pallas_call(
        kernel,
        out_shape=[jax.ShapeDtypeStruct(s, jnp.float32) for s in outs],
        in_specs=in_specs,
        out_specs=out_specs,
        scratch_shapes=scratch,
        compiler_params=pltpu.CompilerParams(vmem_limit_bytes=vmem),
        cost_estimate=pl.CostEstimate(flops=moved * 1000, bytes_accessed=moved, transcendentals=0),
    )(*args)


def density_kernel(chunks, occ_in, orb, parts, occ, u, dens, sems):
    size = ROWS // chunks
    loads = [pltpu.make_async_copy(occ_in, occ, sems.at[0]), pltpu.make_async_copy(orb, u, sems.at[1])]
    for c in loads:
        c.start()
    for c in loads:
        c.wait()

    def plane(p, _):
        total = occ[0] * u[0, p] * u[0, p]
        for o in range(1, NB):
            total = total + occ[o] * u[o, p] * u[o, p]
        dens[pl.ds(pl.multiple_of(p * NY, NY), NY), :] = total
        return 0

    lax.fori_loop(0, BX, plane, 0, unroll=2)
    for c in range(chunks):
        parts[c] = dens[pl.ds(c * size, size), :]


def density(chunks, occ, orb):
    def kernel(*refs):
        density_kernel(chunks, *refs)

    return call(
        kernel,
        [(chunks, ROWS // chunks, NZ)],
        [HBM, HBM],
        [VM],
        [
            pltpu.SMEM((NB,), jnp.float32),
            pltpu.VMEM((NB, BX, NY, NZ), jnp.float32),
            pltpu.VMEM((ROWS, NZ), jnp.float32),
            pltpu.SemaphoreType.DMA((2,)),
        ],
        (occ, orb),
        vmem=VMEM_ALL,
    )[0]


def pack_kernel(orb, field, diel, core, packed, u, sems):
    loads = [
        pltpu.make_async_copy(orb, u.at[pl.ds(0, NB)], sems.at[0]),
        pltpu.make_async_copy(field, u.at[NB], sems.at[1]),
        pltpu.make_async_copy(diel, u.at[NB + 1], sems.at[2]),
        pltpu.make_async_copy(core, u.at[NB + 2], sems.at[3]),
    ]
    for c in loads:
        c.start()
    for c in loads:
        c.wait()
    save = pltpu.make_async_copy(u, packed, sems.at[4])
    save.start()
    save.wait()


def pack(orb, field, diel, core):
    return call(
        pack_kernel,
        [(NB + 3, BX, NY, NZ)],
        [HBM] * 4,
        [HBM],
        [pltpu.VMEM((NB + 3, BX, NY, NZ), jnp.float32), pltpu.SemaphoreType.DMA((5,))],
        (orb, field, diel, core),
        moved=BESIDE_FAR,
        vmem=VMEM_ALL,
    )[0]


def spread_kernel(mine, other, out):
    value = mine[...] + other[...]
    for c in range(out.shape[0]):
        out[c] = value


def spread(chunks, mine, other):
    return call(
        spread_kernel,
        [(chunks, *mine.shape)],
        [VM, VM],
        [VM],
        [],
        (mine, other),
        moved=BESIDE_NEAR,
    )[0]


def join_kernel(chunks, got, left, right, to_right, to_left, sems):
    size = ROWS // chunks
    copies = []
    for at, (src, edge, dst) in enumerate(
        (
            (left, BX - 1, to_right),
            (right, 0, to_left),
        )
    ):
        for k in range(2):
            copies.append(
                pltpu.make_async_copy(
                    src.at[NB + k, edge],
                    dst.at[pl.ds(ROWS + k * NY, NY)],
                    sems.at[2 * at + k],
                )
            )
    for c in copies:
        c.start()
    for c in range(chunks):
        value = got[c]
        for dst in (to_right, to_left):
            dst[pl.ds(c * size, size), :] = value
    for c in copies:
        c.wait()


def join(chunks, got, left, right):
    def kernel(*refs):
        join_kernel(chunks, *refs)

    return call(
        kernel,
        [(ROWS + 2 * NY, NZ), (ROWS + 2 * NY, NZ)],
        [VM, ANY, ANY],
        [VM, VM],
        [pltpu.SemaphoreType.DMA((4,))],
        (got, left, right),
    )


def strips(ref, *at):
    return [ref[(*at, pl.ds(j, STRIPS, stride=NV), slice(None))] for j in range(NV)]


def put_strips(ref, values, *at):
    for j, value in enumerate(values):
        ref[(*at, pl.ds(j, STRIPS, stride=NV), slice(None))] = value


def plain(ref, *at):
    return [ref[(*at, j)] for j in range(NV)]


def put_plain(ref, values, *at):
    for j, value in enumerate(values):
        ref[(*at, j)] = value


class Masks:
    def __init__(self):
        self.lane = lax.broadcasted_iota(jnp.int32, (STRIPS, NZ), 1)
        self.row = lax.broadcasted_iota(jnp.int32, (STRIPS, NZ), 0)


def with_sides(mid, count, m):
    before = [jnp.where(m.row >= 1, pltpu.roll(mid[NV - count + k], 1, 0), 0.0) for k in range(count)]
    after = [jnp.where(m.row < STRIPS - 1, pltpu.roll(mid[k], STRIPS - 1, 0), 0.0) for k in range(count)]
    return before + mid + after


def band_matrix():
    row = lax.broadcasted_iota(jnp.int32, (2 * NZ, NZ), 0)
    apart = jnp.abs(jnp.where(row >= NZ, row - NZ, row) - lax.broadcasted_iota(jnp.int32, (2 * NZ, NZ), 1))
    value = jnp.zeros((2 * NZ, NZ), jnp.float32)
    for dist, weight in zip((1, 2, 3), COEFFS):
        value = jnp.where(apart == dist, float(round(180.0 * weight)), value)
    return value.astype(jnp.bfloat16)


def along_z(x, matrix):
    high = x.astype(jnp.bfloat16)
    low = (x - high.astype(jnp.float32)).astype(jnp.bfloat16)
    return jnp.dot(jnp.concatenate([high, low], axis=1), matrix, preferred_element_type=jnp.float32)


def stencil(get, zs, m, factor):
    mid = get(0)
    wide = with_sides(mid, 3, m)
    totals = [(factor * SCALE / 180.0) * z for z in zs]
    for dist, weight in zip((1, 2, 3), COEFFS):
        up, down = get(dist), get(-dist)
        for j in range(NV):
            along = (up[j] + down[j]) + (wide[3 + j + dist] + wide[3 + j - dist])
            totals[j] = totals[j] + (factor * SCALE * weight) * along
    return totals, mid


def face_sums(d, xp, xm, keep, m):
    wide = with_sides(d, 1, m)
    not_last = m.lane < NZ - 1
    not_begin = m.lane >= 1
    out = []
    for j in range(NV):
        ahead = jnp.where(not_last, pltpu.roll(d[j], NZ - 1, 1), 0.0)
        behind = jnp.where(not_begin, pltpu.roll(d[j], 1, 1), 0.0)
        sums = [d[j] + v for v in (xp[j], xm[j], wide[j + 2], wide[j], ahead, behind)]
        den = ((sums[0] + sums[1]) + (sums[2] + sums[3])) + (sums[4] + sums[5])
        inverse = jnp.where(keep, 1.0 / den, 0.0)
        sums[4] = jnp.where(not_last, sums[4], 0.0)
        sums[5] = jnp.where(not_begin, sums[5], 0.0)
        out.append([s * inverse for s in sums] + [8.0 * inverse])
    return out


def weigh_kernel(edges, diel, field, left, right, wts, fs, ds):
    m = Masks()
    for k, (lo, own, hi) in enumerate(((left.at[NB], field, right.at[NB]), (left.at[NB + 1], diel, right.at[NB + 1]))):
        dst = (fs, ds)[k]

        def move(p, _):
            put_plain(dst, strips(lo, p), p)
            put_plain(dst, strips(own, p), p + BX)
            put_plain(dst, strips(hi, p), p + 2 * BX)
            return 0

        lax.fori_loop(0, BX, move, 0)
    has_left = edges[0] > 0
    has_right = edges[1] > 0

    def weigh(i, _):
        keep = ((i >= BX - 1) | has_left) & ((i < 2 * BX - 1) | has_right)
        got = face_sums(plain(ds, i + 1), plain(ds, i + 2), plain(ds, i), keep, m)
        for j in range(NV):
            for k in range(7):
                wts[k, i, j] = got[j][k]
        return 0

    lax.fori_loop(0, 3 * BX - 2, weigh, 0, unroll=2)


def weigh(edges, diel, field, left, right):
    vec = (NV, STRIPS, NZ)
    return call(
        weigh_kernel,
        [(7, 3 * BX - 2, *vec), (3 * BX, *vec)],
        [SM] + [VM] * 4,
        [VM, VM],
        [pltpu.VMEM((3 * BX, *vec), jnp.float32)],
        (edges, diel, field, left, right),
    )


def first_kernel(
    edges, orb, core, left, right, mine, rho_left, rho_right, wts, fs,
    potential, y1, y2, diag,
    fa, fb, src, xc, zp,
):
    has_left = edges[0] > 0
    has_right = edges[1] > 0
    m = Masks()
    matrix = band_matrix()

    for o in range(NB):
        for ref, lo, count, at in ((left, BX - 3, 3, 0), (orb, 0, BX, 3), (right, 0, 3, 3 + BX)):
            x = ref[o, pl.ds(lo, count)].reshape(count * NY, NZ)
            zp[o, pl.ds(at, count)] = along_z(x, matrix).reshape(count, NY, NZ)

    def sources(ref, lo, hi, base):
        def body(p, _):
            i = p + base
            for j, v in enumerate(strips(ref, p)):
                src[i, j] = wts[6, i, j] * v
            return 0

        lax.fori_loop(lo, hi, body, 0)

    sources(rho_left, 1, BX, -1)
    sources(mine, 0, BX, BX - 1)
    sources(rho_right, 0, BX - 1, 2 * BX - 1)

    def exchange(ref, extra, lo, count, base):
        def body(p, _):
            for j, (a, b) in enumerate(zip(strips(ref, p + lo), strips(extra, p + lo))):
                x = a + b
                x = jnp.where(x > 0.0, x, 1.0)
                root = jnp.exp(jnp.log(x) * (1.0 / 3.0))
                root = root - (root - x / (root * root)) * (1.0 / 3.0)
                xc[p + base, j] = SLATER * root
            return 0

        lax.fori_loop(0, count, body, 0)

    exchange(rho_left, left.at[NB + 2], BX - 3, 3, 0)
    exchange(mine, core, 0, BX, 3)
    exchange(rho_right, right.at[NB + 2], 0, 3, 3 + BX)

    def swept(mid, up, down, w, s):
        wide = with_sides(mid, 1, m)
        out = []
        for j in range(NV):
            total = w(0, j) * up[j] + w(1, j) * down[j]
            total = total + (w(2, j) * wide[j + 2] + w(3, j) * wide[j])
            total = total + (w(4, j) * pltpu.roll(mid[j], NZ - 1, 1) + w(5, j) * pltpu.roll(mid[j], 1, 1))
            out.append(total + s(j))
        return out

    for near, far, rho, sign in ((left, rho_left, rho_left, 1), (right, rho_right, rho_right, -1)):
        p = 0 if sign > 0 else BX - 1
        e = p if sign > 0 else 3 * BX - 1
        inner, outer = strips(near, NB + 1, p + sign), strips(far, BX + 1)
        xp, xm = (inner, outer) if sign > 0 else (outer, inner)
        got = face_sums(strips(near, NB + 1, p), xp, xm, has_left if sign > 0 else has_right, m)
        f_in, f_out = plain(fs, e + sign), strips(far, BX)
        up, down = (f_in, f_out) if sign > 0 else (f_out, f_in)
        dens = strips(rho, p)
        new = swept(plain(fs, e), up, down, lambda k, j: got[j][k], lambda j: got[j][6] * dens[j])
        put_plain(fb, new, e)

    def sweep(ref, dst, margin):
        def body(e, _):
            new = swept(
                plain(ref, e), plain(ref, e + 1), plain(ref, e - 1),
                lambda k, j: wts[k, e - 1, j], lambda j: src[e - 1, j],
            )
            put_plain(dst, new, e)
            return 0

        lax.fori_loop(margin, 3 * BX - margin, body, 0, unroll=4)

    sweep(fs, fb, 1)
    sweep(fb, fa, 1)
    sweep(fa, fb, 2)

    def last_sweep(j, _):
        e = j + 3
        new = swept(
            plain(fb, e), plain(fb, e + 1), plain(fb, e - 1),
            lambda k, i: wts[k, e - 1, i], lambda i: src[e - 1, i] + xc[j, i],
        )
        put_plain(fa, new, e)
        put_plain(diag, [(v - CENTER) * (1.0 / HALF) + 3.0 * COEFF_ZERO * SCALE for v in new], j)
        return 0

    lax.fori_loop(0, 2 * BX, last_sweep, 0, unroll=2)

    def give(p, _):
        put_strips(potential, plain(fa, p + BX), p)
        return 0

    lax.fori_loop(0, BX, give, 0, unroll=2)

    def step_one(o, _):
        def get(p):
            if p < BX:
                return strips(left, o, p)
            return strips(orb, o, p - BX) if p < 2 * BX else strips(right, o, p - 2 * BX)

        for j in range(2 * BX):
            rest, mid = stencil(lambda dist: get(j + 3 + dist), strips(zp, o, j), m, 1.0)
            new = [a * b + c for a, b, c in zip(plain(diag, j), mid, rest)]
            if j < 3:
                new = [jnp.where(has_left, v, 0.0) for v in new]
            if j >= 3 + BX:
                new = [jnp.where(has_right, v, 0.0) for v in new]
            put_plain(y1, new, o, j)
        return 0

    lax.fori_loop(0, NB, step_one, 0)
    for o in range(NB):
        x = y1[o, pl.ds(3, BX)].reshape(BX * NY, NZ)
        zp[o, pl.ds(0, BX)] = along_z(x, matrix).reshape(BX, NY, NZ)

    def step_two(j, _):
        q = plain(diag, j + 3)
        for o in range(NB):
            zs = [zp[o, j, pl.ds(i * STRIPS, STRIPS), :] for i in range(NV)]
            rest, mid = stencil(lambda dist: plain(y1, o, j + 3 + dist), zs, m, 2.0)
            old = strips(orb, o, j)
            put_plain(y2, [2.0 * a * b + (c - d) for a, b, c, d in zip(q, mid, rest, old)], o, j)
        return 0

    lax.fori_loop(0, BX, step_two, 0)


def first(edges, orb, core, left, right, mine, rho_left, rho_right, wts, fs):
    f = jnp.float32
    vec = (NV, STRIPS, NZ)
    return call(
        first_kernel,
        [(BX, NY, NZ), (NB, 2 * BX, *vec), (NB, BX, *vec), (2 * BX, *vec)],
        [SM] + [VM] * 9,
        [VM, VM, VM, VM],
        [
            pltpu.VMEM((3 * BX, *vec), f),
            pltpu.VMEM((3 * BX, *vec), f),
            pltpu.VMEM((3 * BX - 2, *vec), f),
            pltpu.VMEM((2 * BX, *vec), f),
            pltpu.VMEM((NB, 2 * BX, NY, NZ), f),
        ],
        (edges, orb, core, left, right, mine, rho_left, rho_right, wts, fs),
    )


def second_kernel(edges, y1, y2, left, right, diag, out, y3, zp, done, sems):
    has_left = edges[0] > 0
    has_right = edges[1] > 0
    m = Masks()
    matrix = band_matrix()
    for o in range(NB):
        for ref, lo, count, at in ((left, BX - 3, 3, 0), (y2, 0, BX, 3), (right, 0, 3, 3 + BX)):
            x = ref[o, pl.ds(lo, count)].reshape(count * NY, NZ)
            zp[o, pl.ds(at, count)] = along_z(x, matrix).reshape(count, NV, STRIPS, NZ)

    def step_three(o, _):
        def get(p):
            if p < BX:
                return plain(left, o, p)
            return plain(y2, o, p - BX) if p < 2 * BX else plain(right, o, p - 2 * BX)

        for j in range(2 * BX):
            rest, mid = stencil(lambda dist: get(j + 3 + dist), plain(zp, o, j), m, 2.0)
            old = plain(y1, o, j)
            new = [2.0 * a * b + (c - d) for a, b, c, d in zip(plain(diag, j), mid, rest, old)]
            if j < 3:
                new = [jnp.where(has_left, v, 0.0) for v in new]
            if j >= 3 + BX:
                new = [jnp.where(has_right, v, 0.0) for v in new]
            put_plain(y3, new, o, j)
        return 0

    lax.fori_loop(0, NB, step_three, 0)
    for o in range(NB):
        x = y3[o, pl.ds(3, BX)].reshape(BX * NY, NZ)
        zp[o, pl.ds(0, BX)] = along_z(x, matrix).reshape(BX, NV, STRIPS, NZ)

    def step_four(o, _):
        for j in range(BX):
            rest, mid = stencil(lambda dist: plain(y3, o, j + 3 + dist), plain(zp, o, j), m, 2.0)
            old = plain(y2, o, j)
            new = [2.0 * a * b + (c - d) for a, b, c, d in zip(plain(diag, j + 3), mid, rest, old)]
            put_strips(done, new, o, j)
        pltpu.make_async_copy(done.at[o], out.at[o], sems.at[o]).start()
        return 0

    lax.fori_loop(0, NB, step_four, 0)
    for o in range(NB):
        pltpu.make_async_copy(done.at[o], out.at[o], sems.at[o]).wait()


def second(edges, y1, y2, left, right, diag):
    f = jnp.float32
    vec = (NV, STRIPS, NZ)
    return call(
        second_kernel,
        [(NB, BX, NY, NZ)],
        [SM] + [VM] * 5,
        [ANY],
        [
            pltpu.VMEM((NB, 2 * BX, *vec), f),
            pltpu.VMEM((NB, 2 * BX, *vec), f),
            pltpu.VMEM((NB, BX, NY, NZ), f),
            pltpu.SemaphoreType.DMA((NB,)),
        ],
        (edges, y1, y2, left, right, diag),
    )[0]


def from_sides(to_right, to_left):
    n = lax.axis_size("dom")
    left = lax.ppermute(to_right, "dom", [(i, i + 1) for i in range(n - 1)])
    right = lax.ppermute(to_left, "dom", [(i + 1, i) for i in range(n - 1)])
    return left, right


def local(orbitals, occupation, dielectric, core_density, start_field):
    bands = lax.axis_size("band")
    dom = lax.axis_index("dom")
    far = bands // 2
    groups = [list(range(far)), list(range(far, bands))]
    edges = jnp.stack([(dom > 0).astype(jnp.int32), (dom < lax.axis_size("dom") - 1).astype(jnp.int32)])

    parts = density(far, occupation, orbitals)
    parts = lax.all_to_all(parts, "band", 0, 0, axis_index_groups=groups)
    mine = jnp.sum(parts, axis=0)
    other = lax.ppermute(mine, "band", [(i, (i + far) % bands) for i in range(bands)])
    held, mine = lax.optimization_barrier(((orbitals, start_field, dielectric, core_density), mine))
    packed = pack(*held)
    left, right = from_sides(packed, packed)
    got = lax.all_to_all(spread(far, mine, other), "band", 0, 0, axis_index_groups=groups)
    to_right, to_left = join(far, got, left, right)
    rho_left, rho_right = from_sides(to_right, to_left)
    (left, right), to_right = lax.optimization_barrier(((left, right), to_right))
    wts, fs = weigh(edges, dielectric, start_field, left, right)
    cells = (-1, NY, NZ)
    potential, y1, y2, diag = first(
        edges, orbitals, core_density, left, right,
        to_right.reshape(cells), rho_left.reshape(cells), rho_right.reshape(cells), wts, fs,
    )
    y2_left, y2_right = from_sides(y2, y2)
    return potential, second(edges, y1, y2, y2_left, y2_right, diag)


def solution(mesh):
    return jax.shard_map(
        local,
        mesh=mesh,
        in_specs=(
            P("band", "dom", None, None),
            P("band"),
            P("dom", None, None),
            P("dom", None, None),
            P("dom", None, None),
        ),
        out_specs=(P("dom", None, None), P("band", "dom", None, None)),
        check_vma=False,
    )
```

```python
import jax
import jax.numpy as jnp
from jax import lax
from jax.experimental import pallas as pl
from jax.experimental.pallas import tpu as pltpu
from jax.sharding import PartitionSpec as P

NB = 4
BX = 6
NY = 48
NZ = 128
ROWS = BX * NY
STRIPS = 8
NV = NY // STRIPS

COEFFS = (1.5, -0.15, 1.0 / 90.0)
COEFF_ZERO = -49.0 / 18.0
CENTER = 5.25
HALF = 4.75
SLATER = -0.9847450218426964
SCALE = -0.5 / HALF

VMEM_LIMIT = 12 * 1024 * 1024
VMEM_ALL = 63 * 1024 * 1024
ANY = pl.BlockSpec(memory_space=pl.ANY)
HBM = pl.BlockSpec(memory_space=pltpu.HBM)
BESIDE_FAR = 20_000_000
BESIDE_NEAR = 80_000_000
VM = pl.BlockSpec(memory_space=pltpu.VMEM)
SM = pl.BlockSpec(memory_space=pltpu.SMEM)


def call(kernel, outs, in_specs, out_specs, scratch, args, moved=2_000_000, vmem=VMEM_LIMIT):
    return pl.pallas_call(
        kernel,
        out_shape=[jax.ShapeDtypeStruct(s, jnp.float32) for s in outs],
        in_specs=in_specs,
        out_specs=out_specs,
        scratch_shapes=scratch,
        compiler_params=pltpu.CompilerParams(vmem_limit_bytes=vmem),
        cost_estimate=pl.CostEstimate(flops=moved * 1000, bytes_accessed=moved, transcendentals=0),
    )(*args)


def density_kernel(chunks, occ_in, orb, parts, occ, u, dens, sems):
    size = ROWS // chunks
    loads = [pltpu.make_async_copy(occ_in, occ, sems.at[0]), pltpu.make_async_copy(orb, u, sems.at[1])]
    for c in loads:
        c.start()
    for c in loads:
        c.wait()

    def plane(p, _):
        total = occ[0] * u[0, p] * u[0, p]
        for o in range(1, NB):
            total = total + occ[o] * u[o, p] * u[o, p]
        dens[pl.ds(pl.multiple_of(p * NY, NY), NY), :] = total
        return 0

    lax.fori_loop(0, BX, plane, 0, unroll=2)
    for c in range(chunks):
        parts[c] = dens[pl.ds(c * size, size), :]


def density(chunks, occ, orb):
    def kernel(*refs):
        density_kernel(chunks, *refs)

    return call(
        kernel,
        [(chunks, ROWS // chunks, NZ)],
        [HBM, HBM],
        [VM],
        [
            pltpu.SMEM((NB,), jnp.float32),
            pltpu.VMEM((NB, BX, NY, NZ), jnp.float32),
            pltpu.VMEM((ROWS, NZ), jnp.float32),
            pltpu.SemaphoreType.DMA((2,)),
        ],
        (occ, orb),
        vmem=VMEM_ALL,
    )[0]


def pack_kernel(orb, field, diel, core, packed, u, sems):
    loads = [
        pltpu.make_async_copy(orb, u.at[pl.ds(0, NB)], sems.at[0]),
        pltpu.make_async_copy(field, u.at[NB], sems.at[1]),
        pltpu.make_async_copy(diel, u.at[NB + 1], sems.at[2]),
        pltpu.make_async_copy(core, u.at[NB + 2], sems.at[3]),
    ]
    for c in loads:
        c.start()
    for c in loads:
        c.wait()
    save = pltpu.make_async_copy(u, packed, sems.at[4])
    save.start()
    save.wait()


def pack(orb, field, diel, core):
    return call(
        pack_kernel,
        [(NB + 3, BX, NY, NZ)],
        [HBM] * 4,
        [HBM],
        [pltpu.VMEM((NB + 3, BX, NY, NZ), jnp.float32), pltpu.SemaphoreType.DMA((5,))],
        (orb, field, diel, core),
        moved=BESIDE_FAR,
        vmem=VMEM_ALL,
    )[0]


def spread_kernel(mine, other, out):
    value = mine[...] + other[...]
    for c in range(out.shape[0]):
        out[c] = value


def spread(chunks, mine, other):
    return call(
        spread_kernel,
        [(chunks, *mine.shape)],
        [VM, VM],
        [VM],
        [],
        (mine, other),
        moved=BESIDE_NEAR,
    )[0]


def join_kernel(chunks, sides, got, far, near, to_near, to_far, sems):
    size = ROWS // chunks
    turn = sides[1]
    copies = []
    for at, (src, edge, dst) in enumerate(((far, BX - 1, to_near), (near, 0, to_far))):
        for k in range(2):
            copies.append(
                pltpu.make_async_copy(
                    src.at[NB + k, turned(turn, edge)],
                    dst.at[pl.ds(ROWS + k * NY, NY)],
                    sems.at[2 * at + k],
                )
            )
    for c in copies:
        c.start()
    for c in range(chunks):
        value = got[c]
        for dst in (to_near, to_far):
            dst[pl.ds(c * size, size), :] = value
    for c in copies:
        c.wait()


def join(chunks, sides, got, near, far):
    def kernel(*refs):
        join_kernel(chunks, *refs)

    return call(
        kernel,
        [(ROWS + 2 * NY, NZ), (ROWS + 2 * NY, NZ)],
        [SM, VM, ANY, ANY],
        [VM, VM],
        [pltpu.SemaphoreType.DMA((4,))],
        (sides, got, far, near),
    )


def turned(turn, p):
    return jnp.where(turn > 0, BX - 1 - p, p)


def strips(ref, *at):
    return [ref[(*at, pl.ds(j, STRIPS, stride=NV), slice(None))] for j in range(NV)]


def put_strips(ref, values, *at):
    for j, value in enumerate(values):
        ref[(*at, pl.ds(j, STRIPS, stride=NV), slice(None))] = value


def plain(ref, *at):
    return [ref[(*at, j)] for j in range(NV)]


def put_plain(ref, values, *at):
    for j, value in enumerate(values):
        ref[(*at, j)] = value


class Masks:
    def __init__(self):
        self.lane = lax.broadcasted_iota(jnp.int32, (STRIPS, NZ), 1)
        self.row = lax.broadcasted_iota(jnp.int32, (STRIPS, NZ), 0)


def with_sides(mid, count, m):
    before = [jnp.where(m.row >= 1, pltpu.roll(mid[NV - count + k], 1, 0), 0.0) for k in range(count)]
    after = [jnp.where(m.row < STRIPS - 1, pltpu.roll(mid[k], STRIPS - 1, 0), 0.0) for k in range(count)]
    return before + mid + after


def band_matrix():
    row = lax.broadcasted_iota(jnp.int32, (2 * NZ, NZ), 0)
    apart = jnp.abs(jnp.where(row >= NZ, row - NZ, row) - lax.broadcasted_iota(jnp.int32, (2 * NZ, NZ), 1))
    value = jnp.zeros((2 * NZ, NZ), jnp.float32)
    for dist, weight in zip((1, 2, 3), COEFFS):
        value = jnp.where(apart == dist, float(round(180.0 * weight)), value)
    return value.astype(jnp.bfloat16)


def along_z(x, matrix):
    high = x.astype(jnp.bfloat16)
    low = (x - high.astype(jnp.float32)).astype(jnp.bfloat16)
    return jnp.dot(jnp.concatenate([high, low], axis=1), matrix, preferred_element_type=jnp.float32)


def stencil(get, zs, m, factor):
    mid = get(0)
    wide = with_sides(mid, 3, m)
    totals = [(factor * SCALE / 180.0) * z for z in zs]
    for dist, weight in zip((1, 2, 3), COEFFS):
        up, down = get(dist), get(-dist)
        for j in range(NV):
            along = (up[j] + down[j]) + (wide[3 + j + dist] + wide[3 + j - dist])
            totals[j] = totals[j] + (factor * SCALE * weight) * along
    return totals, mid


def face_sums(d, xp, xm, keep, m):
    wide = with_sides(d, 1, m)
    not_last = m.lane < NZ - 1
    not_begin = m.lane >= 1
    out = []
    for j in range(NV):
        ahead = jnp.where(not_last, pltpu.roll(d[j], NZ - 1, 1), 0.0)
        behind = jnp.where(not_begin, pltpu.roll(d[j], 1, 1), 0.0)
        sums = [d[j] + v for v in (xp[j], xm[j], wide[j + 2], wide[j], ahead, behind)]
        den = ((sums[0] + sums[1]) + (sums[2] + sums[3])) + (sums[4] + sums[5])
        inverse = 1.0 / den if keep is None else jnp.where(keep, 1.0 / den, 0.0)
        sums[4] = jnp.where(not_last, sums[4], 0.0)
        sums[5] = jnp.where(not_begin, sums[5], 0.0)
        out.append([s * inverse for s in sums] + [8.0 * inverse])
    return out


def weigh_kernel(sides, diel, field, far, near, wts, fs, ds):
    m = Masks()
    turn = sides[1]
    for k, (lo, own, hi) in enumerate(((far.at[NB], field, near.at[NB]), (far.at[NB + 1], diel, near.at[NB + 1]))):
        dst = (fs, ds)[k]

        def move(p, _):
            put_plain(dst, strips(lo, turned(turn, p)), p)
            put_plain(dst, strips(own, turned(turn, p)), p + BX)
            put_plain(dst, strips(hi, turned(turn, p)), p + 2 * BX)
            return 0

        lax.fori_loop(0, BX, move, 0)
    has_far = sides[0] > 0

    def weigh(i, _):
        keep = (i >= BX - 1) | has_far
        got = face_sums(plain(ds, i + 1), plain(ds, i + 2), plain(ds, i), keep, m)
        for j in range(NV):
            for k in range(7):
                wts[k, i, j] = got[j][k]
        return 0

    lax.fori_loop(0, 3 * BX - 2, weigh, 0, unroll=2)


def weigh(sides, diel, field, far, near):
    vec = (NV, STRIPS, NZ)
    return call(
        weigh_kernel,
        [(7, 3 * BX - 2, *vec), (3 * BX, *vec)],
        [SM] + [VM] * 4,
        [VM, VM],
        [pltpu.VMEM((3 * BX, *vec), jnp.float32)],
        (sides, diel, field, far, near),
    )


def first_kernel(
    sides, orb, core, far, near, mine, rho_far, rho_near, wts, fs,
    potential, y1, y2, diag,
    fa, fb, src, xc, zp,
):
    has_far = sides[0] > 0
    turn = sides[1]
    at = [turned(turn, p) for p in range(BX)]
    m = Masks()
    matrix = band_matrix()

    for o in range(NB):
        for ref, planes, base in ((far, (3, 4, 5), 0), (orb, range(BX), 3), (near, (0, 1, 2), 3 + BX)):
            x = jnp.concatenate([ref[o, at[p]] for p in planes], axis=0)
            zp[o, pl.ds(base, len(planes))] = along_z(x, matrix).reshape(len(planes), NY, NZ)

    def sources(ref, lo, hi, base):
        def body(p, _):
            i = p + base
            for j, v in enumerate(strips(ref, turned(turn, p))):
                src[i, j] = wts[6, i, j] * v
            return 0

        lax.fori_loop(lo, hi, body, 0)

    sources(rho_far, 1, BX, -1)
    sources(mine, 0, BX, BX - 1)
    sources(rho_near, 0, BX - 1, 2 * BX - 1)

    def exchange(ref, extra, lo, count, base):
        def body(p, _):
            plane = turned(turn, p + lo)
            for j, (a, b) in enumerate(zip(strips(ref, plane), strips(extra, plane))):
                x = a + b
                x = jnp.where(x > 0.0, x, 1.0)
                root = jnp.exp(jnp.log(x) * (1.0 / 3.0))
                root = root - (root - x / (root * root)) * (1.0 / 3.0)
                xc[p + base, j] = SLATER * root
            return 0

        lax.fori_loop(0, count, body, 0)

    exchange(rho_far, far.at[NB + 2], BX - 3, 3, 0)
    exchange(mine, core, 0, BX, 3)
    exchange(rho_near, near.at[NB + 2], 0, 3, 3 + BX)

    def swept(mid, up, down, w, s):
        wide = with_sides(mid, 1, m)
        out = []
        for j in range(NV):
            total = w(0, j) * up[j] + w(1, j) * down[j]
            total = total + (w(2, j) * wide[j + 2] + w(3, j) * wide[j])
            total = total + (w(4, j) * pltpu.roll(mid[j], NZ - 1, 1) + w(5, j) * pltpu.roll(mid[j], 1, 1))
            out.append(total + s(j))
        return out

    for brick, rho, sign in ((far, rho_far, 1), (near, rho_near, -1)):
        p = 0 if sign > 0 else BX - 1
        e = p if sign > 0 else 3 * BX - 1
        inner, outer = strips(brick, NB + 1, at[p + sign]), strips(rho, BX + 1)
        xp, xm = (inner, outer) if sign > 0 else (outer, inner)
        got = face_sums(strips(brick, NB + 1, at[p]), xp, xm, has_far if sign > 0 else None, m)
        f_in, f_out = plain(fs, e + sign), strips(rho, BX)
        up, down = (f_in, f_out) if sign > 0 else (f_out, f_in)
        dens = strips(rho, at[p])
        new = swept(plain(fs, e), up, down, lambda k, j: got[j][k], lambda j: got[j][6] * dens[j])
        put_plain(fb, new, e)

    def sweep(ref, dst, margin):
        def body(e, _):
            new = swept(
                plain(ref, e), plain(ref, e + 1), plain(ref, e - 1),
                lambda k, j: wts[k, e - 1, j], lambda j: src[e - 1, j],
            )
            put_plain(dst, new, e)
            return 0

        lax.fori_loop(margin, 3 * BX - margin, body, 0, unroll=4)

    sweep(fs, fb, 1)
    sweep(fb, fa, 1)
    sweep(fa, fb, 2)

    def last_sweep(j, _):
        e = j + 3
        new = swept(
            plain(fb, e), plain(fb, e + 1), plain(fb, e - 1),
            lambda k, i: wts[k, e - 1, i], lambda i: src[e - 1, i] + xc[j, i],
        )
        put_plain(fa, new, e)
        put_plain(diag, [(v - CENTER) * (1.0 / HALF) + 3.0 * COEFF_ZERO * SCALE for v in new], j)
        return 0

    lax.fori_loop(0, 2 * BX, last_sweep, 0, unroll=2)

    def give(p, _):
        put_strips(potential, plain(fa, p + BX), turned(turn, p))
        return 0

    lax.fori_loop(0, BX, give, 0, unroll=2)

    def step_one(o, _):
        def get(p):
            return strips((far, orb, near)[p // BX], o, at[p % BX])

        for j in range(2 * BX):
            rest, mid = stencil(lambda dist: get(j + 3 + dist), strips(zp, o, j), m, 1.0)
            new = [a * b + c for a, b, c in zip(plain(diag, j), mid, rest)]
            if j < 3:
                new = [jnp.where(has_far, v, 0.0) for v in new]
            put_plain(y1, new, o, j)
        return 0

    lax.fori_loop(0, NB, step_one, 0)
    for o in range(NB):
        x = y1[o, pl.ds(3, BX)].reshape(BX * NY, NZ)
        zp[o, pl.ds(0, BX)] = along_z(x, matrix).reshape(BX, NY, NZ)

    def step_two(j, _):
        q = plain(diag, j + 3)
        for o in range(NB):
            zs = [zp[o, j, pl.ds(i * STRIPS, STRIPS), :] for i in range(NV)]
            rest, mid = stencil(lambda dist: plain(y1, o, j + 3 + dist), zs, m, 2.0)
            here = turned(turn, j)
            old = strips(orb, o, here)
            put_plain(y2, [2.0 * a * b + (c - d) for a, b, c, d in zip(q, mid, rest, old)], o, here)
        return 0

    lax.fori_loop(0, BX, step_two, 0)


def first(sides, orb, core, far, near, mine, rho_far, rho_near, wts, fs):
    f = jnp.float32
    vec = (NV, STRIPS, NZ)
    return call(
        first_kernel,
        [(BX, NY, NZ), (NB, 2 * BX, *vec), (NB, BX, *vec), (2 * BX, *vec)],
        [SM] + [VM] * 9,
        [VM, VM, VM, VM],
        [
            pltpu.VMEM((3 * BX, *vec), f),
            pltpu.VMEM((3 * BX, *vec), f),
            pltpu.VMEM((3 * BX - 2, *vec), f),
            pltpu.VMEM((2 * BX, *vec), f),
            pltpu.VMEM((NB, 2 * BX, NY, NZ), f),
        ],
        (sides, orb, core, far, near, mine, rho_far, rho_near, wts, fs),
    )


def second_kernel(sides, y1, y2, near, far, diag, out, y3, zp, done, sems):
    has_far = sides[0] > 0
    turn = sides[1]
    at = [turned(turn, p) for p in range(BX)]
    m = Masks()
    matrix = band_matrix()
    for o in range(NB):
        for ref, planes, base in ((far, (3, 4, 5), 0), (y2, range(BX), 3), (near, (0, 1, 2), 3 + BX)):
            x = jnp.concatenate([ref[o, at[p]].reshape(NY, NZ) for p in planes], axis=0)
            zp[o, pl.ds(base, len(planes))] = along_z(x, matrix).reshape(len(planes), NV, STRIPS, NZ)

    def step_three(o, _):
        def get(p):
            return plain((far, y2, near)[p // BX], o, at[p % BX])

        for j in range(2 * BX):
            rest, mid = stencil(lambda dist: get(j + 3 + dist), plain(zp, o, j), m, 2.0)
            old = plain(y1, o, j)
            new = [2.0 * a * b + (c - d) for a, b, c, d in zip(plain(diag, j), mid, rest, old)]
            if j < 3:
                new = [jnp.where(has_far, v, 0.0) for v in new]
            put_plain(y3, new, o, j)
        return 0

    lax.fori_loop(0, NB, step_three, 0)
    for o in range(NB):
        x = y3[o, pl.ds(3, BX)].reshape(BX * NY, NZ)
        zp[o, pl.ds(0, BX)] = along_z(x, matrix).reshape(BX, NV, STRIPS, NZ)

    def step_four(o, _):
        for j in range(BX):
            rest, mid = stencil(lambda dist: plain(y3, o, j + 3 + dist), plain(zp, o, j), m, 2.0)
            old = plain(y2, o, at[j])
            new = [2.0 * a * b + (c - d) for a, b, c, d in zip(plain(diag, j + 3), mid, rest, old)]
            put_strips(done, new, o, at[j])
        pltpu.make_async_copy(done.at[o], out.at[o], sems.at[o]).start()
        return 0

    lax.fori_loop(0, NB, step_four, 0)
    for o in range(NB):
        pltpu.make_async_copy(done.at[o], out.at[o], sems.at[o]).wait()


def second(sides, y1, y2, far, near, diag):
    f = jnp.float32
    vec = (NV, STRIPS, NZ)
    return call(
        second_kernel,
        [(NB, BX, NY, NZ)],
        [SM] + [VM] * 5,
        [ANY],
        [
            pltpu.VMEM((NB, 2 * BX, *vec), f),
            pltpu.VMEM((NB, 2 * BX, *vec), f),
            pltpu.VMEM((NB, BX, NY, NZ), f),
            pltpu.SemaphoreType.DMA((NB,)),
        ],
        (sides, y1, y2, near, far, diag),
    )[0]


def swapped(to_far, to_near):
    n = lax.axis_size("dom")
    pairs = [(i, i + 1) for i in range(n - 1)]
    far = [p for i, j in pairs if i % 2 for p in ((i, j), (j, i))]
    near = [p for i, j in pairs if i % 2 == 0 for p in ((i, j), (j, i))]
    return lax.ppermute(to_far, "dom", far), lax.ppermute(to_near, "dom", near)


def local(orbitals, occupation, dielectric, core_density, start_field):
    bands = lax.axis_size("band")
    dom = lax.axis_index("dom")
    half = bands // 2
    groups = [list(range(half)), list(range(half, bands))]
    turn = dom % 2
    has_far = jnp.where(turn > 0, dom < lax.axis_size("dom") - 1, dom > 0)
    sides = jnp.stack([has_far.astype(jnp.int32), turn.astype(jnp.int32)])

    parts = density(half, occupation, orbitals)
    parts = lax.all_to_all(parts, "band", 0, 0, axis_index_groups=groups)
    mine = jnp.sum(parts, axis=0)
    other = lax.ppermute(mine, "band", [(i, (i + half) % bands) for i in range(bands)])
    held, mine = lax.optimization_barrier(((orbitals, start_field, dielectric, core_density), mine))
    packed = pack(*held)
    far, near = swapped(packed, packed)
    got = lax.all_to_all(spread(half, mine, other), "band", 0, 0, axis_index_groups=groups)
    to_near, to_far = join(half, sides, got, near, far)
    rho_far, rho_near = swapped(to_far, to_near)
    (far, near), to_near = lax.optimization_barrier(((far, near), to_near))
    wts, fs = weigh(sides, dielectric, start_field, far, near)
    cells = (-1, NY, NZ)
    potential, y1, y2, diag = first(
        sides, orbitals, core_density, far, near,
        to_near.reshape(cells), rho_far.reshape(cells), rho_near.reshape(cells), wts, fs,
    )
    y2_far, y2_near = swapped(y2, y2)
    return potential, second(sides, y1, y2, y2_far, y2_near, diag)


def solution(mesh):
    return jax.shard_map(
        local,
        mesh=mesh,
        in_specs=(
            P("band", "dom", None, None),
            P("band"),
            P("dom", None, None),
            P("dom", None, None),
            P("dom", None, None),
        ),
        out_specs=(P("dom", None, None), P("band", "dom", None, None)),
        check_vma=False,
    )
```

```python
import jax
import jax.numpy as jnp
from jax import lax
from jax.experimental import pallas as pl
from jax.experimental.pallas import tpu as pltpu
from jax.sharding import PartitionSpec as P

NB = 4
BX = 6
NY = 48
NZ = 128
ROWS = BX * NY
STRIPS = 8
NV = NY // STRIPS
VEC = (NV, STRIPS, NZ)

COEFFS = (1.5, -0.15, 1.0 / 90.0)
COEFF_ZERO = -49.0 / 18.0
CENTER = 5.25
HALF = 4.75
SLATER = -0.9847450218426964
SCALE = -0.5 / HALF

VMEM_LIMIT = 12 * 1024 * 1024
VMEM_ALL = 63 * 1024 * 1024
ANY = pl.BlockSpec(memory_space=pl.ANY)
HBM = pl.BlockSpec(memory_space=pltpu.HBM)
BESIDE_FAR = 20_000_000
BESIDE_NEAR = 80_000_000
VM = pl.BlockSpec(memory_space=pltpu.VMEM)
SM = pl.BlockSpec(memory_space=pltpu.SMEM)


def call(kernel, outs, in_specs, out_specs, scratch, args, moved=2_000_000, vmem=VMEM_LIMIT, aliases=None):
    return pl.pallas_call(
        kernel,
        out_shape=[jax.ShapeDtypeStruct(s, jnp.float32) for s in outs],
        in_specs=in_specs,
        out_specs=out_specs,
        scratch_shapes=scratch,
        input_output_aliases=aliases or {},
        compiler_params=pltpu.CompilerParams(vmem_limit_bytes=vmem),
        cost_estimate=pl.CostEstimate(flops=moved * 1000, bytes_accessed=moved, transcendentals=0),
    )(*args)


def density_kernel(chunks, occ_in, orb, parts, occ, u, dens, sems):
    size = ROWS // chunks
    loads = [pltpu.make_async_copy(occ_in, occ, sems.at[0]), pltpu.make_async_copy(orb, u, sems.at[1])]
    for c in loads:
        c.start()
    for c in loads:
        c.wait()

    def plane(p, _):
        total = occ[0] * u[0, p] * u[0, p]
        for o in range(1, NB):
            total = total + occ[o] * u[o, p] * u[o, p]
        dens[pl.ds(pl.multiple_of(p * NY, NY), NY), :] = total
        return 0

    lax.fori_loop(0, BX, plane, 0, unroll=2)
    for c in range(chunks):
        parts[c] = dens[pl.ds(c * size, size), :]


def density(chunks, occ, orb):
    def kernel(*refs):
        density_kernel(chunks, *refs)

    return call(
        kernel,
        [(chunks, ROWS // chunks, NZ)],
        [HBM, HBM],
        [VM],
        [
            pltpu.SMEM((NB,), jnp.float32),
            pltpu.VMEM((NB, BX, NY, NZ), jnp.float32),
            pltpu.VMEM((ROWS, NZ), jnp.float32),
            pltpu.SemaphoreType.DMA((2,)),
        ],
        (occ, orb),
        vmem=VMEM_ALL,
    )[0]


def pack_kernel(orb, field, diel, core, packed, u, sems):
    loads = [
        pltpu.make_async_copy(orb, u.at[pl.ds(0, NB)], sems.at[0]),
        pltpu.make_async_copy(field, u.at[NB], sems.at[1]),
        pltpu.make_async_copy(diel, u.at[NB + 1], sems.at[2]),
        pltpu.make_async_copy(core, u.at[NB + 2], sems.at[3]),
    ]
    for c in loads:
        c.start()
    for c in loads:
        c.wait()
    save = pltpu.make_async_copy(u, packed, sems.at[4])
    save.start()
    save.wait()


def pack(orb, field, diel, core):
    return call(
        pack_kernel,
        [(NB + 3, BX, NY, NZ)],
        [HBM] * 4,
        [HBM],
        [pltpu.VMEM((NB + 3, BX, NY, NZ), jnp.float32), pltpu.SemaphoreType.DMA((5,))],
        (orb, field, diel, core),
        moved=BESIDE_FAR,
        vmem=VMEM_ALL,
    )[0]


def spread_kernel(mine, other, out):
    value = mine[...] + other[...]
    for c in range(out.shape[0]):
        out[c] = value


def spread(chunks, mine, other):
    return call(
        spread_kernel,
        [(chunks, *mine.shape)],
        [VM, VM],
        [VM],
        [],
        (mine, other),
        moved=BESIDE_NEAR,
    )[0]


def join_kernel(chunks, sides, got, far, near, to_near, to_far):
    size = ROWS // chunks
    turn = sides[1]
    for src, edge, dst in ((far, BX - 1, to_near), (near, 0, to_far)):
        for k in range(2):
            dst[pl.ds(ROWS + k * NY, NY), :] = src[NB + k, turned(turn, edge)]
    for c in range(chunks):
        value = got[c]
        for dst in (to_near, to_far):
            dst[pl.ds(c * size, size), :] = value


def join(chunks, sides, got, near, far):
    def kernel(*refs):
        join_kernel(chunks, *refs)

    return call(
        kernel,
        [(ROWS + 2 * NY, NZ), (ROWS + 2 * NY, NZ)],
        [SM, VM, VM, VM],
        [VM, VM],
        [],
        (sides, got, far, near),
    )


def turned(turn, p):
    return jnp.where(turn > 0, BX - 1 - p, p)


def strips(ref, *at):
    return [ref[(*at, pl.ds(j, STRIPS, stride=NV), slice(None))] for j in range(NV)]


def put_strips(ref, values, *at):
    for j, value in enumerate(values):
        ref[(*at, pl.ds(j, STRIPS, stride=NV), slice(None))] = value


def plain(ref, *at):
    return [ref[(*at, j)] for j in range(NV)]


def put_plain(ref, values, *at):
    for j, value in enumerate(values):
        ref[(*at, j)] = value


class Masks:
    def __init__(self):
        self.lane = lax.broadcasted_iota(jnp.int32, (STRIPS, NZ), 1)
        self.row = lax.broadcasted_iota(jnp.int32, (STRIPS, NZ), 0)


def with_sides(mid, count, m):
    before = [jnp.where(m.row >= 1, pltpu.roll(mid[NV - count + k], 1, 0), 0.0) for k in range(count)]
    after = [jnp.where(m.row < STRIPS - 1, pltpu.roll(mid[k], STRIPS - 1, 0), 0.0) for k in range(count)]
    return before + mid + after


def band_matrix():
    row = lax.broadcasted_iota(jnp.int32, (2 * NZ, NZ), 0)
    apart = jnp.abs(jnp.where(row >= NZ, row - NZ, row) - lax.broadcasted_iota(jnp.int32, (2 * NZ, NZ), 1))
    value = jnp.zeros((2 * NZ, NZ), jnp.float32)
    for dist, weight in zip((1, 2, 3), COEFFS):
        value = jnp.where(apart == dist, float(round(180.0 * weight)), value)
    return value.astype(jnp.bfloat16)


def along_z(x, matrix):
    high = x.astype(jnp.bfloat16)
    low = (x - high.astype(jnp.float32)).astype(jnp.bfloat16)
    return jnp.dot(jnp.concatenate([high, low], axis=1), matrix, preferred_element_type=jnp.float32)


def stencil(get, zs, m, factor):
    mid = get(0)
    wide = with_sides(mid, 3, m)
    totals = [(factor * SCALE / 180.0) * z for z in zs]
    for dist, weight in zip((1, 2, 3), COEFFS):
        planes = [p for p in (get(dist), get(-dist)) if p is not None]
        for j in range(NV):
            along = wide[3 + j + dist] + wide[3 + j - dist]
            for p in planes:
                along = along + p[j]
            totals[j] = totals[j] + (factor * SCALE * weight) * along
    return totals, mid


def face_sums(d, xp, xm, keep, m):
    wide = with_sides(d, 1, m)
    not_last = m.lane < NZ - 1
    not_begin = m.lane >= 1
    out = []
    for j in range(NV):
        ahead = jnp.where(not_last, pltpu.roll(d[j], NZ - 1, 1), 0.0)
        behind = jnp.where(not_begin, pltpu.roll(d[j], 1, 1), 0.0)
        sums = [d[j] + v for v in (xp[j], xm[j], wide[j + 2], wide[j], ahead, behind)]
        den = ((sums[0] + sums[1]) + (sums[2] + sums[3])) + (sums[4] + sums[5])
        inverse = 1.0 / den if keep is None else jnp.where(keep, 1.0 / den, 0.0)
        sums[4] = jnp.where(not_last, sums[4], 0.0)
        sums[5] = jnp.where(not_begin, sums[5], 0.0)
        out.append([s * inverse for s in sums] + [8.0 * inverse])
    return out


def extended(bricks, o, at):
    def get(p):
        return strips(bricks[p // BX], o, at[p % BX])

    return get


def prepare_kernel(sides, orb, diel, field, far, near, wts, fs, rest, ds, zp):
    m = Masks()
    matrix = band_matrix()
    has_far = sides[0] > 0
    turn = sides[1]
    at = [turned(turn, p) for p in range(BX)]
    for o in range(NB):
        for ref, planes, base in ((far, (3, 4, 5), 0), (orb, range(BX), 3), (near, (0, 1, 2), 3 + BX)):
            x = jnp.concatenate([ref[o, at[p]] for p in planes], axis=0)
            zp[o, pl.ds(base, len(planes))] = along_z(x, matrix).reshape(len(planes), NY, NZ)
    for k, (lo, own, hi) in enumerate(((far.at[NB], field, near.at[NB]), (far.at[NB + 1], diel, near.at[NB + 1]))):
        dst = (fs, ds)[k]

        def move(p, _):
            put_plain(dst, strips(lo, turned(turn, p)), p)
            put_plain(dst, strips(own, turned(turn, p)), p + BX)
            put_plain(dst, strips(hi, turned(turn, p)), p + 2 * BX)
            return 0

        lax.fori_loop(0, BX, move, 0)

    def weigh(i, _):
        keep = (i >= BX - 1) | has_far
        got = face_sums(plain(ds, i + 1), plain(ds, i + 2), plain(ds, i), keep, m)
        for j in range(NV):
            for k in range(7):
                wts[k, i, j] = got[j][k]
        return 0

    lax.fori_loop(0, 3 * BX - 2, weigh, 0, unroll=2)

    def laplace(o, _):
        get = extended((far, orb, near), o, at)
        for j in range(2 * BX):
            total, _ = stencil(lambda dist: get(j + 3 + dist), strips(zp, o, j), m, 1.0)
            put_plain(rest, total, o, j)
        return 0

    lax.fori_loop(0, NB, laplace, 0)


def prepare(sides, orb, diel, field, far, near):
    return call(
        prepare_kernel,
        [(7, 3 * BX - 2, *VEC), (3 * BX, *VEC), (NB, 2 * BX, *VEC)],
        [SM] + [VM] * 5,
        [VM] * 3,
        [pltpu.VMEM((3 * BX, *VEC), jnp.float32), pltpu.VMEM((NB, 2 * BX, NY, NZ), jnp.float32)],
        (sides, orb, diel, field, far, near),
    )


def two_steps(sides, orb, far, near, diag, rest, y1, y2, zp, m):
    has_far = sides[0] > 0
    turn = sides[1]
    at = [turned(turn, p) for p in range(BX)]
    matrix = band_matrix()

    def step_one(i, _):
        get = extended((far, orb, near), i, at)
        for j in range(2 * BX):
            new = [a * b + c for a, b, c in zip(plain(diag, j), get(j + 3), plain(rest, i, j))]
            if j < 3:
                new = [jnp.where(has_far, v, 0.0) for v in new]
            put_plain(y1, new, i, j)
        return 0

    lax.fori_loop(0, NB, step_one, 0)
    for i in range(NB):
        x = y1[i, pl.ds(3, BX)].reshape(BX * NY, NZ)
        zp[i] = along_z(x, matrix).reshape(BX, *VEC)

    def step_two(j, _):
        q = plain(diag, j + 3)
        here = turned(turn, j)
        for i in range(NB):
            part, mid = stencil(lambda dist: plain(y1, i, j + 3 + dist), plain(zp, i, j), m, 2.0)
            old = strips(orb, i, here)
            put_plain(y2, [2.0 * a * b + (c - d) for a, b, c, d in zip(q, mid, part, old)], i, here)
        return 0

    lax.fori_loop(0, BX, step_two, 0)


def first_kernel(
    sides, orb, core, far, near, mine, rho_far, rho_near, wts, fs, rest,
    potential, diag, y1, y2,
    fa, fb, src, xc, zp,
):
    has_far = sides[0] > 0
    turn = sides[1]
    at = [turned(turn, p) for p in range(BX)]
    m = Masks()

    def sources(ref, lo, hi, base):
        def body(p, _):
            i = p + base
            for j, v in enumerate(strips(ref, turned(turn, p))):
                src[i, j] = wts[6, i, j] * v
            return 0

        lax.fori_loop(lo, hi, body, 0)

    sources(rho_far, 1, BX, -1)
    sources(mine, 0, BX, BX - 1)
    sources(rho_near, 0, BX - 1, 2 * BX - 1)

    def exchange(ref, extra, lo, count, base):
        def body(p, _):
            plane = turned(turn, p + lo)
            for j, (a, b) in enumerate(zip(strips(ref, plane), strips(extra, plane))):
                x = a + b
                x = jnp.where(x > 0.0, x, 1.0)
                root = jnp.exp(jnp.log(x) * (1.0 / 3.0))
                root = root - (root - x / (root * root)) * (1.0 / 3.0)
                xc[p + base, j] = SLATER * root
            return 0

        lax.fori_loop(0, count, body, 0)

    exchange(rho_far, far.at[NB + 2], BX - 3, 3, 0)
    exchange(mine, core, 0, BX, 3)
    exchange(rho_near, near.at[NB + 2], 0, 3, 3 + BX)

    def swept(mid, up, down, w, s):
        wide = with_sides(mid, 1, m)
        out = []
        for j in range(NV):
            total = w(0, j) * up[j] + w(1, j) * down[j]
            total = total + (w(2, j) * wide[j + 2] + w(3, j) * wide[j])
            total = total + (w(4, j) * pltpu.roll(mid[j], NZ - 1, 1) + w(5, j) * pltpu.roll(mid[j], 1, 1))
            out.append(total + s(j))
        return out

    for brick, rho, sign in ((far, rho_far, 1), (near, rho_near, -1)):
        p = 0 if sign > 0 else BX - 1
        e = p if sign > 0 else 3 * BX - 1
        inner, outer = strips(brick, NB + 1, at[p + sign]), strips(rho, BX + 1)
        xp, xm = (inner, outer) if sign > 0 else (outer, inner)
        got = face_sums(strips(brick, NB + 1, at[p]), xp, xm, has_far if sign > 0 else None, m)
        f_in, f_out = plain(fs, e + sign), strips(rho, BX)
        up, down = (f_in, f_out) if sign > 0 else (f_out, f_in)
        dens = strips(rho, at[p])
        new = swept(plain(fs, e), up, down, lambda k, j: got[j][k], lambda j: got[j][6] * dens[j])
        put_plain(fb, new, e)

    def sweep(ref, dst, margin):
        def body(e, _):
            new = swept(
                plain(ref, e), plain(ref, e + 1), plain(ref, e - 1),
                lambda k, j: wts[k, e - 1, j], lambda j: src[e - 1, j],
            )
            put_plain(dst, new, e)
            return 0

        lax.fori_loop(margin, 3 * BX - margin, body, 0, unroll=4)

    sweep(fs, fb, 1)
    sweep(fb, fa, 1)
    sweep(fa, fb, 2)

    def last_sweep(j, _):
        e = j + 3
        new = swept(
            plain(fb, e), plain(fb, e + 1), plain(fb, e - 1),
            lambda k, i: wts[k, e - 1, i], lambda i: src[e - 1, i] + xc[j, i],
        )
        put_plain(fa, new, e)
        put_plain(diag, [(v - CENTER) * (1.0 / HALF) + 3.0 * COEFF_ZERO * SCALE for v in new], j)
        return 0

    lax.fori_loop(0, 2 * BX, last_sweep, 0, unroll=4)

    def give(p, _):
        put_strips(potential, plain(fa, p + BX), turned(turn, p))
        return 0

    lax.fori_loop(0, BX, give, 0, unroll=2)
    two_steps(sides, orb, far, near, diag, rest, y1, y2, zp, m)


def first(sides, orb, core, far, near, mine, rho_far, rho_near, wts, fs, rest):
    f = jnp.float32
    return call(
        first_kernel,
        [(BX, NY, NZ), (2 * BX, *VEC), (NB, 2 * BX, *VEC), (NB, BX, *VEC)],
        [SM] + [VM] * 10,
        [VM] * 4,
        [
            pltpu.VMEM((3 * BX, *VEC), f),
            pltpu.VMEM((3 * BX, *VEC), f),
            pltpu.VMEM((3 * BX - 2, *VEC), f),
            pltpu.VMEM((2 * BX, *VEC), f),
            pltpu.VMEM((NB, BX, *VEC), f),
        ],
        (sides, orb, core, far, near, mine, rho_far, rho_near, wts, fs, rest),
    )


def own_kernel(y1, y2, diag, turn_in, partial, zp):
    turn = turn_in[1]
    at = [turned(turn, p) for p in range(BX)]
    m = Masks()
    matrix = band_matrix()
    for o in range(NB):
        x = jnp.concatenate([y2[o, at[p]].reshape(NY, NZ) for p in range(BX)], axis=0)
        zp[o] = along_z(x, matrix).reshape(BX, *VEC)

    def step_three(o, _):
        for j in range(BX):
            part, mid = stencil(
                lambda dist: plain(y2, o, at[j + dist]) if 0 <= j + dist < BX else None, plain(zp, o, j), m, 2.0
            )
            old = plain(y1, o, j + 3)
            new = [2.0 * a * b + (c - d) for a, b, c, d in zip(plain(diag, j + 3), mid, part, old)]
            put_plain(partial, new, o, j)
        return 0

    lax.fori_loop(0, NB, step_three, 0)


def own(sides, y1, y2, diag):
    return call(
        own_kernel,
        [(NB, BX, *VEC)],
        [VM] * 3 + [SM],
        [VM],
        [pltpu.VMEM((NB, BX, *VEC), jnp.float32)],
        (y1, y2, diag, sides),
    )[0]


def last_kernel(sides, y1, y2, near, far, diag, partial, out, y3, zp, done, sems):
    has_far = sides[0] > 0
    turn = sides[1]
    at = [turned(turn, p) for p in range(BX)]
    m = Masks()
    matrix = band_matrix()
    for o in range(NB):
        for ref, planes, base in ((far, (3, 4, 5), 0), (near, (0, 1, 2), 3)):
            x = jnp.concatenate([ref[o, at[p]].reshape(NY, NZ) for p in planes], axis=0)
            zp[o, pl.ds(base, 3)] = along_z(x, matrix).reshape(3, *VEC)

    def step_three(o, _):
        def get(p):
            return plain((far, y2, near)[p // BX], o, at[p % BX])

        for j in (0, 1, 2, BX + 3, BX + 4, BX + 5):
            part, mid = stencil(lambda dist: get(j + 3 + dist), plain(zp, o, j if j < 3 else j - BX), m, 2.0)
            old = plain(y1, o, j)
            new = [2.0 * a * b + (c - d) for a, b, c, d in zip(plain(diag, j), mid, part, old)]
            if j < 3:
                new = [jnp.where(has_far, v, 0.0) for v in new]
            put_plain(y3, new, o, j)
        for j in range(BX):
            new = plain(partial, o, j)
            for dist, weight in zip((1, 2, 3), COEFFS):
                for p in (j - dist, j + dist):
                    if not 0 <= p < BX:
                        new = [a + (2.0 * SCALE * weight) * b for a, b in zip(new, get(p + BX))]
            put_plain(y3, new, o, j + 3)
        return 0

    lax.fori_loop(0, NB, step_three, 0)
    for o in range(NB):
        x = y3[o, pl.ds(3, BX)].reshape(BX * NY, NZ)
        zp[o] = along_z(x, matrix).reshape(BX, *VEC)

    def step_four(o, _):
        for j in range(BX):
            part, mid = stencil(lambda dist: plain(y3, o, j + 3 + dist), plain(zp, o, j), m, 2.0)
            old = plain(y2, o, at[j])
            new = [2.0 * a * b + (c - d) for a, b, c, d in zip(plain(diag, j + 3), mid, part, old)]
            put_strips(done, new, o, at[j])
        pltpu.make_async_copy(done.at[o], out.at[o], sems.at[o]).start()
        return 0

    lax.fori_loop(0, NB, step_four, 0)
    for o in range(NB):
        pltpu.make_async_copy(done.at[o], out.at[o], sems.at[o]).wait()


def last(sides, y1, y2, near, far, diag, partial):
    f = jnp.float32
    return call(
        last_kernel,
        [(NB, BX, NY, NZ)],
        [SM] + [VM] * 6,
        [HBM],
        [
            pltpu.VMEM((NB, 2 * BX, *VEC), f),
            pltpu.VMEM((NB, BX, *VEC), f),
            pltpu.VMEM((NB, BX, NY, NZ), f),
            pltpu.SemaphoreType.DMA((NB,)),
        ],
        (sides, y1, y2, near, far, diag, partial),
    )[0]


def swap_far(x):
    n = lax.axis_size("dom")
    return lax.ppermute(x, "dom", [p for i in range(1, n - 1, 2) for p in ((i, i + 1), (i + 1, i))])


def swap_near(x):
    n = lax.axis_size("dom")
    return lax.ppermute(x, "dom", [p for i in range(0, n - 1, 2) for p in ((i, i + 1), (i + 1, i))])


def local(orbitals, occupation, dielectric, core_density, start_field):
    bands = lax.axis_size("band")
    dom = lax.axis_index("dom")
    half = bands // 2
    groups = [list(range(half)), list(range(half, bands))]
    turn = dom % 2
    has_far = jnp.where(turn > 0, dom < lax.axis_size("dom") - 1, dom > 0)
    sides = jnp.stack([has_far.astype(jnp.int32), turn.astype(jnp.int32)])

    parts = density(half, occupation, orbitals)
    held, parts = lax.optimization_barrier(((orbitals, start_field, dielectric, core_density), parts))
    packed = pack(*held)
    parts = lax.all_to_all(parts, "band", 0, 0, axis_index_groups=groups)
    mine = jnp.sum(parts, axis=0)
    mine, packed = lax.optimization_barrier((mine, packed))
    other = lax.ppermute(mine, "band", [(i, (i + half) % bands) for i in range(bands)])
    far, near = swap_far(packed), swap_near(packed)
    got = lax.all_to_all(spread(half, mine, other), "band", 0, 0, axis_index_groups=groups)
    to_near, to_far = join(half, sides, got, far, near)
    rho_far, rho_near = swap_far(to_far), swap_near(to_near)
    (far, near), to_near = lax.optimization_barrier(((far, near), to_near))
    wts, fs, rest = prepare(sides, orbitals, dielectric, start_field, far, near)
    cells = (-1, NY, NZ)
    potential, diag, y1, y2 = first(
        sides, orbitals, core_density, far, near,
        to_near.reshape(cells), rho_far.reshape(cells), rho_near.reshape(cells), wts, fs, rest,
    )
    y2_far, y2_near = swap_far(y2), swap_near(y2)
    partial = own(sides, y1, y2, diag)
    return potential, last(sides, y1, y2, y2_near, y2_far, diag, partial)


def solution(mesh):
    return jax.shard_map(
        local,
        mesh=mesh,
        in_specs=(
            P("band", "dom", None, None),
            P("band"),
            P("dom", None, None),
            P("dom", None, None),
            P("dom", None, None),
        ),
        out_specs=(P("dom", None, None), P("band", "dom", None, None)),
        check_vma=False,
    )
```

```python
import jax
import jax.numpy as jnp
from jax import lax
from jax.experimental import pallas as pl
from jax.experimental.pallas import tpu as pltpu
from jax.sharding import PartitionSpec as P

NB = 4
BX = 6
NY = 48
NZ = 128
ROWS = BX * NY
STRIPS = 8
NV = NY // STRIPS
VEC = (NV, STRIPS, NZ)

COEFFS = (1.5, -0.15, 1.0 / 90.0)
COEFF_ZERO = -49.0 / 18.0
CENTER = 5.25
HALF = 4.75
SLATER = -0.9847450218426964
SCALE = -0.5 / HALF

VMEM_LIMIT = 12 * 1024 * 1024
VMEM_ALL = 63 * 1024 * 1024
ANY = pl.BlockSpec(memory_space=pl.ANY)
HBM = pl.BlockSpec(memory_space=pltpu.HBM)
BESIDE_FAR = 20_000_000
BESIDE_NEAR = 80_000_000
VM = pl.BlockSpec(memory_space=pltpu.VMEM)
SM = pl.BlockSpec(memory_space=pltpu.SMEM)


def call(kernel, outs, in_specs, out_specs, scratch, args, moved=2_000_000, vmem=VMEM_LIMIT, aliases=None):
    return pl.pallas_call(
        kernel,
        out_shape=[jax.ShapeDtypeStruct(s, jnp.float32) for s in outs],
        in_specs=in_specs,
        out_specs=out_specs,
        scratch_shapes=scratch,
        input_output_aliases=aliases or {},
        compiler_params=pltpu.CompilerParams(vmem_limit_bytes=vmem),
        cost_estimate=pl.CostEstimate(flops=moved * 1000, bytes_accessed=moved, transcendentals=0),
    )(*args)


def density_kernel(chunks, occ_in, orb, parts, occ, u, dens, held, sems):
    size = ROWS // chunks
    load_occ = pltpu.make_async_copy(occ_in, occ, sems.at[0])
    load_occ.start()
    half = BX // 2
    loads, saves = [], []
    for h in range(2):
        planes = pl.ds(h * half, half)
        loads.append(pltpu.make_async_copy(orb.at[:, planes], u.at[:, planes], sems.at[1 + h]))
        loads[h].start()
        some = pl.ds(h * chunks // 2, chunks // 2)
        saves.append(pltpu.make_async_copy(held.at[some], parts.at[some], sems.at[3 + h]))
    load_occ.wait()

    def plane(p, _):
        total = occ[0] * u[0, p] * u[0, p]
        for o in range(1, NB):
            total = total + occ[o] * u[o, p] * u[o, p]
        dens[pl.ds(pl.multiple_of(p * NY, NY), NY), :] = total
        return 0

    for h in range(2):
        loads[h].wait()
        lax.fori_loop(h * half, (h + 1) * half, plane, 0, unroll=True)
        for c in range(h * chunks // 2, (h + 1) * chunks // 2):
            held[c] = dens[pl.ds(c * size, size), :]
        saves[h].start()
    for c in saves:
        c.wait()


def density(chunks, occ, orb):
    def kernel(*refs):
        density_kernel(chunks, *refs)

    return call(
        kernel,
        [(chunks, ROWS // chunks, NZ)],
        [HBM, HBM],
        [HBM],
        [
            pltpu.SMEM((NB,), jnp.float32),
            pltpu.VMEM((NB, BX, NY, NZ), jnp.float32),
            pltpu.VMEM((ROWS, NZ), jnp.float32),
            pltpu.VMEM((chunks, ROWS // chunks, NZ), jnp.float32),
            pltpu.SemaphoreType.DMA((5,)),
        ],
        (occ, orb),
        vmem=VMEM_ALL,
    )[0]


def pack_kernel(orb, field, diel, core, packed, u, sems):
    loads = [
        pltpu.make_async_copy(orb, u.at[pl.ds(0, NB)], sems.at[0]),
        pltpu.make_async_copy(field, u.at[NB], sems.at[1]),
        pltpu.make_async_copy(diel, u.at[NB + 1], sems.at[2]),
        pltpu.make_async_copy(core, u.at[NB + 2], sems.at[3]),
    ]
    for c in loads:
        c.start()
    for c in loads:
        c.wait()
    save = pltpu.make_async_copy(u, packed, sems.at[4])
    save.start()
    save.wait()


def pack(orb, field, diel, core):
    return call(
        pack_kernel,
        [(NB + 3, BX, NY, NZ)],
        [HBM] * 4,
        [HBM],
        [pltpu.VMEM((NB + 3, BX, NY, NZ), jnp.float32), pltpu.SemaphoreType.DMA((5,))],
        (orb, field, diel, core),
        moved=BESIDE_FAR,
        vmem=VMEM_ALL,
    )[0]


def spread_kernel(mine, other, out):
    value = mine[...] + other[...]
    for c in range(out.shape[0]):
        out[c] = value


def spread(chunks, mine, other):
    return call(
        spread_kernel,
        [(chunks, *mine.shape)],
        [VM, VM],
        [VM],
        [],
        (mine, other),
        moved=BESIDE_NEAR,
    )[0]


def join_kernel(chunks, sides, got, far, near, to_near, to_far):
    size = ROWS // chunks
    turn = sides[1]
    for src, edge, dst in ((far, BX - 1, to_near), (near, 0, to_far)):
        for k in range(2):
            dst[pl.ds(ROWS + k * NY, NY), :] = src[NB + k, turned(turn, edge)]
    for c in range(chunks):
        value = got[c]
        for dst in (to_near, to_far):
            dst[pl.ds(c * size, size), :] = value


def join(chunks, sides, got, near, far):
    def kernel(*refs):
        join_kernel(chunks, *refs)

    return call(
        kernel,
        [(ROWS + 2 * NY, NZ), (ROWS + 2 * NY, NZ)],
        [SM, VM, VM, VM],
        [VM, VM],
        [],
        (sides, got, far, near),
    )


def turned(turn, p):
    return jnp.where(turn > 0, BX - 1 - p, p)


def strips(ref, *at):
    return [ref[(*at, pl.ds(j, STRIPS, stride=NV), slice(None))] for j in range(NV)]


def put_strips(ref, values, *at):
    for j, value in enumerate(values):
        ref[(*at, pl.ds(j, STRIPS, stride=NV), slice(None))] = value


def plain(ref, *at):
    return [ref[(*at, j)] for j in range(NV)]


def put_plain(ref, values, *at):
    for j, value in enumerate(values):
        ref[(*at, j)] = value


class Masks:
    def __init__(self):
        self.lane = lax.broadcasted_iota(jnp.int32, (STRIPS, NZ), 1)
        self.row = lax.broadcasted_iota(jnp.int32, (STRIPS, NZ), 0)


def with_sides(mid, count, m):
    before = [jnp.where(m.row >= 1, pltpu.roll(mid[NV - count + k], 1, 0), 0.0) for k in range(count)]
    after = [jnp.where(m.row < STRIPS - 1, pltpu.roll(mid[k], STRIPS - 1, 0), 0.0) for k in range(count)]
    return before + mid + after


def band_matrix():
    row = lax.broadcasted_iota(jnp.int32, (2 * NZ, NZ), 0)
    apart = jnp.abs(jnp.where(row >= NZ, row - NZ, row) - lax.broadcasted_iota(jnp.int32, (2 * NZ, NZ), 1))
    value = jnp.zeros((2 * NZ, NZ), jnp.float32)
    for dist, weight in zip((1, 2, 3), COEFFS):
        value = jnp.where(apart == dist, float(round(180.0 * weight)), value)
    return value.astype(jnp.bfloat16)


def along_z(x, matrix):
    high = x.astype(jnp.bfloat16)
    low = (x - high.astype(jnp.float32)).astype(jnp.bfloat16)
    return jnp.dot(jnp.concatenate([high, low], axis=1), matrix, preferred_element_type=jnp.float32)


def stencil(get, zs, m, factor):
    mid = get(0)
    wide = with_sides(mid, 3, m)
    totals = [(factor * SCALE / 180.0) * z for z in zs]
    for dist, weight in zip((1, 2, 3), COEFFS):
        planes = [p for p in (get(dist), get(-dist)) if p is not None]
        for j in range(NV):
            along = wide[3 + j + dist] + wide[3 + j - dist]
            for p in planes:
                along = along + p[j]
            totals[j] = totals[j] + (factor * SCALE * weight) * along
    return totals, mid


def face_sums(d, xp, xm, keep, m):
    wide = with_sides(d, 1, m)
    not_last = m.lane < NZ - 1
    not_begin = m.lane >= 1
    out = []
    for j in range(NV):
        ahead = jnp.where(not_last, pltpu.roll(d[j], NZ - 1, 1), 0.0)
        behind = jnp.where(not_begin, pltpu.roll(d[j], 1, 1), 0.0)
        sums = [d[j] + v for v in (xp[j], xm[j], wide[j + 2], wide[j], ahead, behind)]
        den = ((sums[0] + sums[1]) + (sums[2] + sums[3])) + (sums[4] + sums[5])
        inverse = 1.0 / den if keep is None else jnp.where(keep, 1.0 / den, 0.0)
        sums[4] = jnp.where(not_last, sums[4], 0.0)
        sums[5] = jnp.where(not_begin, sums[5], 0.0)
        out.append([s * inverse for s in sums] + [8.0 * inverse])
    return out


def extended(bricks, o, at):
    def get(p):
        return strips(bricks[p // BX], o, at[p % BX])

    return get


def prepare_kernel(sides, orb, diel, field, far, near, wts, fs, rest, ds, zp):
    m = Masks()
    matrix = band_matrix()
    has_far = sides[0] > 0
    turn = sides[1]
    at = [turned(turn, p) for p in range(BX)]
    for o in range(NB):
        for ref, planes, base in ((far, (3, 4, 5), 0), (orb, range(BX), 3), (near, (0, 1, 2), 3 + BX)):
            x = jnp.concatenate([ref[o, at[p]] for p in planes], axis=0)
            zp[o, pl.ds(base, len(planes))] = along_z(x, matrix).reshape(len(planes), NY, NZ)
    for k, (lo, own, hi) in enumerate(((far.at[NB], field, near.at[NB]), (far.at[NB + 1], diel, near.at[NB + 1]))):
        dst = (fs, ds)[k]

        def move(p, _):
            put_plain(dst, strips(lo, turned(turn, p)), p)
            put_plain(dst, strips(own, turned(turn, p)), p + BX)
            put_plain(dst, strips(hi, turned(turn, p)), p + 2 * BX)
            return 0

        lax.fori_loop(0, BX, move, 0)

    def weigh(i, _):
        keep = (i >= BX - 1) | has_far
        got = face_sums(plain(ds, i + 1), plain(ds, i + 2), plain(ds, i), keep, m)
        for j in range(NV):
            for k in range(7):
                wts[k, i, j] = got[j][k]
        return 0

    lax.fori_loop(0, 3 * BX - 2, weigh, 0, unroll=4)

    def laplace(o, _):
        get = extended((far, orb, near), o, at)
        for j in range(2 * BX):
            total, _ = stencil(lambda dist: get(j + 3 + dist), strips(zp, o, j), m, 1.0)
            put_plain(rest, total, o, j)
        return 0

    lax.fori_loop(0, NB, laplace, 0)


def prepare(sides, orb, diel, field, far, near):
    return call(
        prepare_kernel,
        [(7, 3 * BX - 2, *VEC), (3 * BX, *VEC), (NB, 2 * BX, *VEC)],
        [SM] + [VM] * 5,
        [VM] * 3,
        [pltpu.VMEM((3 * BX, *VEC), jnp.float32), pltpu.VMEM((NB, 2 * BX, NY, NZ), jnp.float32)],
        (sides, orb, diel, field, far, near),
    )


def two_steps(sides, orb, far, near, diag, rest, y1, y2, zp, m):
    has_far = sides[0] > 0
    turn = sides[1]
    at = [turned(turn, p) for p in range(BX)]
    matrix = band_matrix()

    def step_one(i, _):
        get = extended((far, orb, near), i, at)
        for j in range(2 * BX):
            new = [a * b + c for a, b, c in zip(plain(diag, j), get(j + 3), plain(rest, i, j))]
            if j < 3:
                new = [jnp.where(has_far, v, 0.0) for v in new]
            put_plain(y1, new, i, j)
        return 0

    lax.fori_loop(0, NB, step_one, 0)
    for i in range(NB):
        x = y1[i, pl.ds(3, BX)].reshape(BX * NY, NZ)
        zp[i] = along_z(x, matrix).reshape(BX, *VEC)

    def step_two(j, _):
        q = plain(diag, j + 3)
        here = turned(turn, j)
        for i in range(NB):
            part, mid = stencil(lambda dist: plain(y1, i, j + 3 + dist), plain(zp, i, j), m, 2.0)
            old = strips(orb, i, here)
            put_plain(y2, [2.0 * a * b + (c - d) for a, b, c, d in zip(q, mid, part, old)], i, here)
        return 0

    lax.fori_loop(0, BX, step_two, 0, unroll=2)


def first_kernel(
    sides, orb, core, far, near, mine, rho_far, rho_near, wts, fs, rest,
    potential, diag, y1, y2,
    fa, fb, src, xc, zp, pot, sem,
):
    has_far = sides[0] > 0
    turn = sides[1]
    at = [turned(turn, p) for p in range(BX)]
    m = Masks()

    def sources(ref, lo, hi, base):
        def body(p, _):
            i = p + base
            for j, v in enumerate(strips(ref, turned(turn, p))):
                src[i, j] = wts[6, i, j] * v
            return 0

        lax.fori_loop(lo, hi, body, 0, unroll=True)

    sources(rho_far, 1, BX, -1)
    sources(mine, 0, BX, BX - 1)
    sources(rho_near, 0, BX - 1, 2 * BX - 1)

    def exchange(ref, extra, lo, count, base):
        def body(p, _):
            plane = turned(turn, p + lo)
            for j, (a, b) in enumerate(zip(strips(ref, plane), strips(extra, plane))):
                x = a + b
                x = jnp.where(x > 0.0, x, 1.0)
                root = jnp.exp(jnp.log(x) * (1.0 / 3.0))
                root = root - (root - x / (root * root)) * (1.0 / 3.0)
                xc[p + base, j] = SLATER * root
            return 0

        lax.fori_loop(0, count, body, 0, unroll=3)

    exchange(rho_far, far.at[NB + 2], BX - 3, 3, 0)
    exchange(mine, core, 0, BX, 3)
    exchange(rho_near, near.at[NB + 2], 0, 3, 3 + BX)

    def swept(mid, up, down, w, s):
        wide = with_sides(mid, 1, m)
        out = []
        for j in range(NV):
            total = w(0, j) * up[j] + w(1, j) * down[j]
            total = total + (w(2, j) * wide[j + 2] + w(3, j) * wide[j])
            total = total + (w(4, j) * pltpu.roll(mid[j], NZ - 1, 1) + w(5, j) * pltpu.roll(mid[j], 1, 1))
            out.append(total + s(j))
        return out

    for brick, rho, sign in ((far, rho_far, 1), (near, rho_near, -1)):
        p = 0 if sign > 0 else BX - 1
        e = p if sign > 0 else 3 * BX - 1
        inner, outer = strips(brick, NB + 1, at[p + sign]), strips(rho, BX + 1)
        xp, xm = (inner, outer) if sign > 0 else (outer, inner)
        got = face_sums(strips(brick, NB + 1, at[p]), xp, xm, has_far if sign > 0 else None, m)
        f_in, f_out = plain(fs, e + sign), strips(rho, BX)
        up, down = (f_in, f_out) if sign > 0 else (f_out, f_in)
        dens = strips(rho, at[p])
        new = swept(plain(fs, e), up, down, lambda k, j: got[j][k], lambda j: got[j][6] * dens[j])
        put_plain(fb, new, e)

    def sweep(ref, dst, margin):
        def body(e, _):
            new = swept(
                plain(ref, e), plain(ref, e + 1), plain(ref, e - 1),
                lambda k, j: wts[k, e - 1, j], lambda j: src[e - 1, j],
            )
            put_plain(dst, new, e)
            return 0

        lax.fori_loop(margin, 3 * BX - margin, body, 0, unroll=8)

    sweep(fs, fb, 1)
    sweep(fb, fa, 1)
    sweep(fa, fb, 2)

    def last_sweep(j, _):
        e = j + 3
        new = swept(
            plain(fb, e), plain(fb, e + 1), plain(fb, e - 1),
            lambda k, i: wts[k, e - 1, i], lambda i: src[e - 1, i] + xc[j, i],
        )
        put_plain(fa, new, e)
        put_plain(diag, [(v - CENTER) * (1.0 / HALF) + 3.0 * COEFF_ZERO * SCALE for v in new], j)
        return 0

    lax.fori_loop(0, 2 * BX, last_sweep, 0, unroll=6)

    def give(p, _):
        put_strips(pot, plain(fa, p + BX), turned(turn, p))
        return 0

    lax.fori_loop(0, BX, give, 0, unroll=2)
    save = pltpu.make_async_copy(pot, potential, sem.at[0])
    save.start()
    two_steps(sides, orb, far, near, diag, rest, y1, y2, zp, m)
    save.wait()


def first(sides, orb, core, far, near, mine, rho_far, rho_near, wts, fs, rest):
    f = jnp.float32
    return call(
        first_kernel,
        [(BX, NY, NZ), (2 * BX, *VEC), (NB, 2 * BX, *VEC), (NB, BX, *VEC)],
        [SM] + [VM] * 10,
        [HBM] + [VM] * 3,
        [
            pltpu.VMEM((3 * BX, *VEC), f),
            pltpu.VMEM((3 * BX, *VEC), f),
            pltpu.VMEM((3 * BX - 2, *VEC), f),
            pltpu.VMEM((2 * BX, *VEC), f),
            pltpu.VMEM((NB, BX, *VEC), f),
            pltpu.VMEM((BX, NY, NZ), f),
            pltpu.SemaphoreType.DMA((1,)),
        ],
        (sides, orb, core, far, near, mine, rho_far, rho_near, wts, fs, rest),
    )


def own_kernel(y1, y2, diag, turn_in, partial, zp):
    turn = turn_in[1]
    at = [turned(turn, p) for p in range(BX)]
    m = Masks()
    matrix = band_matrix()
    for o in range(NB):
        x = jnp.concatenate([y2[o, at[p]].reshape(NY, NZ) for p in range(BX)], axis=0)
        zp[o] = along_z(x, matrix).reshape(BX, *VEC)

    def step_three(o, _):
        for j in range(BX):
            part, mid = stencil(
                lambda dist: plain(y2, o, at[j + dist]) if 0 <= j + dist < BX else None, plain(zp, o, j), m, 2.0
            )
            old = plain(y1, o, j + 3)
            new = [2.0 * a * b + (c - d) for a, b, c, d in zip(plain(diag, j + 3), mid, part, old)]
            put_plain(partial, new, o, j)
        return 0

    lax.fori_loop(0, NB, step_three, 0)


def own(sides, y1, y2, diag):
    return call(
        own_kernel,
        [(NB, BX, *VEC)],
        [VM] * 3 + [SM],
        [VM],
        [pltpu.VMEM((NB, BX, *VEC), jnp.float32)],
        (y1, y2, diag, sides),
    )[0]


def last_kernel(sides, y1, y2, near, far, diag, partial, out, y3, zp, done, sems):
    has_far = sides[0] > 0
    turn = sides[1]
    at = [turned(turn, p) for p in range(BX)]
    m = Masks()
    matrix = band_matrix()
    for o in range(NB):
        for ref, planes, base in ((far, (3, 4, 5), 0), (near, (0, 1, 2), 3)):
            x = jnp.concatenate([ref[o, at[p]].reshape(NY, NZ) for p in planes], axis=0)
            zp[o, pl.ds(base, 3)] = along_z(x, matrix).reshape(3, *VEC)

    def step_three(o, _):
        def get(p):
            return plain((far, y2, near)[p // BX], o, at[p % BX])

        for j in (0, 1, 2, BX + 3, BX + 4, BX + 5):
            part, mid = stencil(lambda dist: get(j + 3 + dist), plain(zp, o, j if j < 3 else j - BX), m, 2.0)
            old = plain(y1, o, j)
            new = [2.0 * a * b + (c - d) for a, b, c, d in zip(plain(diag, j), mid, part, old)]
            if j < 3:
                new = [jnp.where(has_far, v, 0.0) for v in new]
            put_plain(y3, new, o, j)
        for j in range(BX):
            new = plain(partial, o, j)
            for dist, weight in zip((1, 2, 3), COEFFS):
                for p in (j - dist, j + dist):
                    if not 0 <= p < BX:
                        new = [a + (2.0 * SCALE * weight) * b for a, b in zip(new, get(p + BX))]
            put_plain(y3, new, o, j + 3)
        return 0

    lax.fori_loop(0, NB, step_three, 0)
    for o in range(NB):
        x = y3[o, pl.ds(3, BX)].reshape(BX * NY, NZ)
        zp[o] = along_z(x, matrix).reshape(BX, *VEC)

    def step_four(o, _):
        for j in range(BX):
            part, mid = stencil(lambda dist: plain(y3, o, j + 3 + dist), plain(zp, o, j), m, 2.0)
            old = plain(y2, o, at[j])
            new = [2.0 * a * b + (c - d) for a, b, c, d in zip(plain(diag, j + 3), mid, part, old)]
            put_strips(done, new, o, at[j])
        pltpu.make_async_copy(done.at[o], out.at[o], sems.at[o]).start()
        return 0

    lax.fori_loop(0, NB, step_four, 0)
    for o in range(NB):
        pltpu.make_async_copy(done.at[o], out.at[o], sems.at[o]).wait()


def last(sides, y1, y2, near, far, diag, partial):
    f = jnp.float32
    return call(
        last_kernel,
        [(NB, BX, NY, NZ)],
        [SM] + [VM] * 6,
        [HBM],
        [
            pltpu.VMEM((NB, 2 * BX, *VEC), f),
            pltpu.VMEM((NB, BX, *VEC), f),
            pltpu.VMEM((NB, BX, NY, NZ), f),
            pltpu.SemaphoreType.DMA((NB,)),
        ],
        (sides, y1, y2, near, far, diag, partial),
    )[0]


def swap_far(x):
    n = lax.axis_size("dom")
    return lax.ppermute(x, "dom", [p for i in range(1, n - 1, 2) for p in ((i, i + 1), (i + 1, i))])


def swap_near(x):
    n = lax.axis_size("dom")
    return lax.ppermute(x, "dom", [p for i in range(0, n - 1, 2) for p in ((i, i + 1), (i + 1, i))])


def local(orbitals, occupation, dielectric, core_density, start_field):
    bands = lax.axis_size("band")
    dom = lax.axis_index("dom")
    half = bands // 2
    groups = [list(range(half)), list(range(half, bands))]
    turn = dom % 2
    has_far = jnp.where(turn > 0, dom < lax.axis_size("dom") - 1, dom > 0)
    sides = jnp.stack([has_far.astype(jnp.int32), turn.astype(jnp.int32)])

    parts = density(half, occupation, orbitals)
    held, parts = lax.optimization_barrier(((orbitals, start_field, dielectric, core_density), parts))
    packed = pack(*held)
    parts = lax.all_to_all(parts, "band", 0, 0, axis_index_groups=groups)
    mine = jnp.sum(parts, axis=0)
    mine, packed = lax.optimization_barrier((mine, packed))
    other = lax.ppermute(mine, "band", [(i, (i + half) % bands) for i in range(bands)])
    far, near = swap_far(packed), swap_near(packed)
    got = lax.all_to_all(spread(half, mine, other), "band", 0, 0, axis_index_groups=groups)
    to_near, to_far = join(half, sides, got, far, near)
    rho_far, rho_near = swap_far(to_far), swap_near(to_near)
    (near, far), to_near = lax.optimization_barrier(((near, far), to_near))
    wts, fs, rest = prepare(sides, orbitals, dielectric, start_field, far, near)
    cells = (-1, NY, NZ)
    potential, diag, y1, y2 = first(
        sides, orbitals, core_density, far, near,
        to_near.reshape(cells), rho_far.reshape(cells), rho_near.reshape(cells), wts, fs, rest,
    )
    y2_far, y2_near = swap_far(y2), swap_near(y2)
    partial = own(sides, y1, y2, diag)
    return potential, last(sides, y1, y2, y2_near, y2_far, diag, partial)


def solution(mesh):
    return jax.shard_map(
        local,
        mesh=mesh,
        in_specs=(
            P("band", "dom", None, None),
            P("band"),
            P("dom", None, None),
            P("dom", None, None),
            P("dom", None, None),
        ),
        out_specs=(P("dom", None, None), P("band", "dom", None, None)),
        check_vma=False,
    )
```

```python
import jax
import jax.numpy as jnp
from jax import lax
from jax.experimental import pallas as pl
from jax.experimental.pallas import tpu as pltpu
from jax.sharding import PartitionSpec as P

NB = 4
BX = 6
NY = 48
NZ = 128
ROWS = BX * NY
STRIPS = 8
NV = NY // STRIPS
VEC = (NV, STRIPS, NZ)

COEFFS = (1.5, -0.15, 1.0 / 90.0)
COEFF_ZERO = -49.0 / 18.0
CENTER = 5.25
HALF = 4.75
SLATER = -0.9847450218426964
SCALE = -0.5 / HALF

VMEM_LIMIT = 12 * 1024 * 1024
VMEM_ALL = 63 * 1024 * 1024
ANY = pl.BlockSpec(memory_space=pl.ANY)
HBM = pl.BlockSpec(memory_space=pltpu.HBM)
BESIDE_FAR = 20_000_000
BESIDE_NEAR = 80_000_000
VM = pl.BlockSpec(memory_space=pltpu.VMEM)
SM = pl.BlockSpec(memory_space=pltpu.SMEM)


def call(kernel, outs, in_specs, out_specs, scratch, args, moved=2_000_000, vmem=VMEM_LIMIT, aliases=None):
    return pl.pallas_call(
        kernel,
        out_shape=[jax.ShapeDtypeStruct(s, jnp.float32) for s in outs],
        in_specs=in_specs,
        out_specs=out_specs,
        scratch_shapes=scratch,
        input_output_aliases=aliases or {},
        compiler_params=pltpu.CompilerParams(vmem_limit_bytes=vmem),
        cost_estimate=pl.CostEstimate(flops=moved * 1000, bytes_accessed=moved, transcendentals=0),
    )(*args)


def density_kernel(chunks, occ_in, orb, parts, occ, u, dens, held, sems):
    size = ROWS // chunks
    load_occ = pltpu.make_async_copy(occ_in, occ, sems.at[0])
    load_occ.start()
    half = BX // 2
    loads, saves = [], []
    for h in range(2):
        planes = pl.ds(h * half, half)
        loads.append(pltpu.make_async_copy(orb.at[:, planes], u.at[:, planes], sems.at[1 + h]))
        loads[h].start()
        some = pl.ds(h * chunks // 2, chunks // 2)
        saves.append(pltpu.make_async_copy(held.at[some], parts.at[some], sems.at[3 + h]))
    load_occ.wait()

    def plane(p, _):
        total = occ[0] * u[0, p] * u[0, p]
        for o in range(1, NB):
            total = total + occ[o] * u[o, p] * u[o, p]
        dens[pl.ds(pl.multiple_of(p * NY, NY), NY), :] = total
        return 0

    for h in range(2):
        loads[h].wait()
        lax.fori_loop(h * half, (h + 1) * half, plane, 0, unroll=True)
        for c in range(h * chunks // 2, (h + 1) * chunks // 2):
            held[c] = dens[pl.ds(c * size, size), :]
        saves[h].start()
    for c in saves:
        c.wait()


def density(chunks, occ, orb):
    def kernel(*refs):
        density_kernel(chunks, *refs)

    return call(
        kernel,
        [(chunks, ROWS // chunks, NZ)],
        [HBM, HBM],
        [HBM],
        [
            pltpu.SMEM((NB,), jnp.float32),
            pltpu.VMEM((NB, BX, NY, NZ), jnp.float32),
            pltpu.VMEM((ROWS, NZ), jnp.float32),
            pltpu.VMEM((chunks, ROWS // chunks, NZ), jnp.float32),
            pltpu.SemaphoreType.DMA((5,)),
        ],
        (occ, orb),
        vmem=VMEM_ALL,
    )[0]


def pack_kernel(orb, field, diel, core, packed, u, sems):
    loads = [
        pltpu.make_async_copy(orb, u.at[pl.ds(0, NB)], sems.at[0]),
        pltpu.make_async_copy(field, u.at[NB], sems.at[1]),
        pltpu.make_async_copy(diel, u.at[NB + 1], sems.at[2]),
        pltpu.make_async_copy(core, u.at[NB + 2], sems.at[3]),
    ]
    for c in loads:
        c.start()
    for c in loads:
        c.wait()
    save = pltpu.make_async_copy(u, packed, sems.at[4])
    save.start()
    save.wait()


def pack(orb, field, diel, core):
    return call(
        pack_kernel,
        [(NB + 3, BX, NY, NZ)],
        [HBM] * 4,
        [HBM],
        [pltpu.VMEM((NB + 3, BX, NY, NZ), jnp.float32), pltpu.SemaphoreType.DMA((5,))],
        (orb, field, diel, core),
        moved=BESIDE_FAR,
        vmem=VMEM_ALL,
    )[0]


def spread_kernel(mine, other, out):
    value = mine[...] + other[...]
    for c in range(out.shape[0]):
        out[c] = value


def spread(chunks, mine, other):
    return call(
        spread_kernel,
        [(chunks, *mine.shape)],
        [VM, VM],
        [VM],
        [],
        (mine, other),
        moved=BESIDE_NEAR,
    )[0]


def join_kernel(chunks, sides, got, far, near, to_near, to_far):
    size = ROWS // chunks
    turn = sides[1]
    for src, edge, dst in ((far, BX - 1, to_near), (near, 0, to_far)):
        for k in range(2):
            dst[pl.ds(ROWS + k * NY, NY), :] = src[NB + k, turned(turn, edge)]
    for c in range(chunks):
        value = got[c]
        for dst in (to_near, to_far):
            dst[pl.ds(c * size, size), :] = value


def join(chunks, sides, got, near, far):
    def kernel(*refs):
        join_kernel(chunks, *refs)

    return call(
        kernel,
        [(ROWS + 2 * NY, NZ), (ROWS + 2 * NY, NZ)],
        [SM, VM, VM, VM],
        [VM, VM],
        [],
        (sides, got, far, near),
    )


def turned(turn, p):
    return jnp.where(turn > 0, BX - 1 - p, p)


def strips(ref, *at):
    return [ref[(*at, pl.ds(j, STRIPS, stride=NV), slice(None))] for j in range(NV)]


def put_strips(ref, values, *at):
    for j, value in enumerate(values):
        ref[(*at, pl.ds(j, STRIPS, stride=NV), slice(None))] = value


def plain(ref, *at):
    return [ref[(*at, j)] for j in range(NV)]


def put_plain(ref, values, *at):
    for j, value in enumerate(values):
        ref[(*at, j)] = value


class Masks:
    def __init__(self):
        self.lane = lax.broadcasted_iota(jnp.int32, (STRIPS, NZ), 1)
        self.row = lax.broadcasted_iota(jnp.int32, (STRIPS, NZ), 0)


def with_sides(mid, count, m):
    before = [jnp.where(m.row >= 1, pltpu.roll(mid[NV - count + k], 1, 0), 0.0) for k in range(count)]
    after = [jnp.where(m.row < STRIPS - 1, pltpu.roll(mid[k], STRIPS - 1, 0), 0.0) for k in range(count)]
    return before + mid + after


def band_matrix():
    row = lax.broadcasted_iota(jnp.int32, (2 * NZ, NZ), 0)
    apart = jnp.abs(jnp.where(row >= NZ, row - NZ, row) - lax.broadcasted_iota(jnp.int32, (2 * NZ, NZ), 1))
    value = jnp.zeros((2 * NZ, NZ), jnp.float32)
    for dist, weight in zip((1, 2, 3), COEFFS):
        value = jnp.where(apart == dist, float(round(180.0 * weight)), value)
    return value.astype(jnp.bfloat16)


def along_z(x, matrix):
    high = x.astype(jnp.bfloat16)
    low = (x - high.astype(jnp.float32)).astype(jnp.bfloat16)
    return jnp.dot(jnp.concatenate([high, low], axis=1), matrix, preferred_element_type=jnp.float32)


def stencil(get, zs, m, factor):
    mid = get(0)
    wide = with_sides(mid, 3, m)
    totals = [(factor * SCALE / 180.0) * z for z in zs]
    for dist, weight in zip((1, 2, 3), COEFFS):
        planes = [p for p in (get(dist), get(-dist)) if p is not None]
        for j in range(NV):
            along = wide[3 + j + dist] + wide[3 + j - dist]
            for p in planes:
                along = along + p[j]
            totals[j] = totals[j] + (factor * SCALE * weight) * along
    return totals, mid


def face_sums(d, xp, xm, keep, m):
    wide = with_sides(d, 1, m)
    not_last = m.lane < NZ - 1
    not_begin = m.lane >= 1
    out = []
    for j in range(NV):
        ahead = jnp.where(not_last, pltpu.roll(d[j], NZ - 1, 1), 0.0)
        behind = jnp.where(not_begin, pltpu.roll(d[j], 1, 1), 0.0)
        sums = [d[j] + v for v in (xp[j], xm[j], wide[j + 2], wide[j], ahead, behind)]
        den = ((sums[0] + sums[1]) + (sums[2] + sums[3])) + (sums[4] + sums[5])
        inverse = 1.0 / den if keep is None else jnp.where(keep, 1.0 / den, 0.0)
        sums[4] = jnp.where(not_last, sums[4], 0.0)
        sums[5] = jnp.where(not_begin, sums[5], 0.0)
        out.append([s * inverse for s in sums] + [8.0 * inverse])
    return out


def extended(bricks, o, at):
    def get(p):
        return strips(bricks[p // BX], o, at[p % BX])

    return get


def prepare_kernel(sides, orb, diel, field, far, near, wts, fs, rest, ds, zp):
    m = Masks()
    matrix = band_matrix()
    has_far = sides[0] > 0
    turn = sides[1]
    at = [turned(turn, p) for p in range(BX)]
    for o in range(NB):
        for ref, planes, base in ((far, (3, 4, 5), 0), (orb, range(BX), 3), (near, (0, 1, 2), 3 + BX)):
            x = jnp.concatenate([ref[o, at[p]] for p in planes], axis=0)
            zp[o, pl.ds(base, len(planes))] = along_z(x, matrix).reshape(len(planes), NY, NZ)
    for k, (lo, own, hi) in enumerate(((far.at[NB], field, near.at[NB]), (far.at[NB + 1], diel, near.at[NB + 1]))):
        dst = (fs, ds)[k]

        def move(p, _):
            put_plain(dst, strips(lo, turned(turn, p)), p)
            put_plain(dst, strips(own, turned(turn, p)), p + BX)
            put_plain(dst, strips(hi, turned(turn, p)), p + 2 * BX)
            return 0

        lax.fori_loop(0, BX, move, 0)

    def weigh(i, _):
        keep = (i >= BX - 1) | has_far
        got = face_sums(plain(ds, i + 1), plain(ds, i + 2), plain(ds, i), keep, m)
        for j in range(NV):
            for k in range(7):
                wts[k, i, j] = got[j][k]
        return 0

    lax.fori_loop(0, 3 * BX - 2, weigh, 0, unroll=4)

    def laplace(o, _):
        get = extended((far, orb, near), o, at)
        for j in range(2 * BX):
            total, _ = stencil(lambda dist: get(j + 3 + dist), strips(zp, o, j), m, 1.0)
            put_plain(rest, total, o, j)
        return 0

    lax.fori_loop(0, NB, laplace, 0)


def prepare(sides, orb, diel, field, far, near):
    return call(
        prepare_kernel,
        [(7, 3 * BX - 2, *VEC), (3 * BX, *VEC), (NB, 2 * BX, *VEC)],
        [SM] + [VM] * 5,
        [VM] * 3,
        [pltpu.VMEM((3 * BX, *VEC), jnp.float32), pltpu.VMEM((NB, 2 * BX, NY, NZ), jnp.float32)],
        (sides, orb, diel, field, far, near),
    )


def two_steps(sides, orb, far, near, diag, rest, y1, y2, zp, m):
    has_far = sides[0] > 0
    turn = sides[1]
    at = [turned(turn, p) for p in range(BX)]
    matrix = band_matrix()

    def step_one(i, _):
        get = extended((far, orb, near), i, at)
        for j in range(2 * BX):
            new = [a * b + c for a, b, c in zip(plain(diag, j), get(j + 3), plain(rest, i, j))]
            if j < 3:
                new = [jnp.where(has_far, v, 0.0) for v in new]
            put_plain(y1, new, i, j)
        return 0

    lax.fori_loop(0, NB, step_one, 0)
    for i in range(NB):
        x = y1[i, pl.ds(3, BX)].reshape(BX * NY, NZ)
        zp[i] = along_z(x, matrix).reshape(BX, *VEC)

    def step_two(j, _):
        q = plain(diag, j + 3)
        here = turned(turn, j)
        for i in range(NB):
            part, mid = stencil(lambda dist: plain(y1, i, j + 3 + dist), plain(zp, i, j), m, 2.0)
            old = strips(orb, i, here)
            put_plain(y2, [2.0 * a * b + (c - d) for a, b, c, d in zip(q, mid, part, old)], i, here)
        return 0

    lax.fori_loop(0, BX, step_two, 0, unroll=2)


def first_kernel(
    sides, orb, core, far, near, mine, rho_far, rho_near, wts, fs, rest,
    potential, diag, y1, y2,
    fa, fb, src, xc, zp, pot, sem,
):
    has_far = sides[0] > 0
    turn = sides[1]
    at = [turned(turn, p) for p in range(BX)]
    m = Masks()

    def sources(ref, lo, hi, base):
        def body(p, _):
            i = p + base
            for j, v in enumerate(strips(ref, turned(turn, p))):
                src[i, j] = wts[6, i, j] * v
            return 0

        lax.fori_loop(lo, hi, body, 0, unroll=True)

    sources(rho_far, 1, BX, -1)
    sources(mine, 0, BX, BX - 1)
    sources(rho_near, 0, BX - 1, 2 * BX - 1)

    def exchange(ref, extra, lo, count, base):
        def body(p, _):
            plane = turned(turn, p + lo)
            for j, (a, b) in enumerate(zip(strips(ref, plane), strips(extra, plane))):
                x = a + b
                x = jnp.where(x > 0.0, x, 1.0)
                root = jnp.exp(jnp.log(x) * (1.0 / 3.0))
                root = root - (root - x / (root * root)) * (1.0 / 3.0)
                xc[p + base, j] = SLATER * root
            return 0

        lax.fori_loop(0, count, body, 0, unroll=3)

    exchange(rho_far, far.at[NB + 2], BX - 3, 3, 0)
    exchange(mine, core, 0, BX, 3)
    exchange(rho_near, near.at[NB + 2], 0, 3, 3 + BX)

    def swept(mid, up, down, w, s):
        wide = with_sides(mid, 1, m)
        out = []
        for j in range(NV):
            total = w(0, j) * up[j] + w(1, j) * down[j]
            total = total + (w(2, j) * wide[j + 2] + w(3, j) * wide[j])
            total = total + (w(4, j) * pltpu.roll(mid[j], NZ - 1, 1) + w(5, j) * pltpu.roll(mid[j], 1, 1))
            out.append(total + s(j))
        return out

    for brick, rho, sign in ((far, rho_far, 1), (near, rho_near, -1)):
        p = 0 if sign > 0 else BX - 1
        e = p if sign > 0 else 3 * BX - 1
        inner, outer = strips(brick, NB + 1, at[p + sign]), strips(rho, BX + 1)
        xp, xm = (inner, outer) if sign > 0 else (outer, inner)
        got = face_sums(strips(brick, NB + 1, at[p]), xp, xm, has_far if sign > 0 else None, m)
        f_in, f_out = plain(fs, e + sign), strips(rho, BX)
        up, down = (f_in, f_out) if sign > 0 else (f_out, f_in)
        dens = strips(rho, at[p])
        new = swept(plain(fs, e), up, down, lambda k, j: got[j][k], lambda j: got[j][6] * dens[j])
        put_plain(fb, new, e)

    def sweep(ref, dst, margin):
        def body(e, _):
            new = swept(
                plain(ref, e), plain(ref, e + 1), plain(ref, e - 1),
                lambda k, j: wts[k, e - 1, j], lambda j: src[e - 1, j],
            )
            put_plain(dst, new, e)
            return 0

        lax.fori_loop(margin, 3 * BX - margin, body, 0, unroll=8)

    sweep(fs, fb, 1)
    sweep(fb, fa, 1)
    sweep(fa, fb, 2)

    def last_sweep(j, _):
        e = j + 3
        new = swept(
            plain(fb, e), plain(fb, e + 1), plain(fb, e - 1),
            lambda k, i: wts[k, e - 1, i], lambda i: src[e - 1, i] + xc[j, i],
        )
        put_plain(fa, new, e)
        put_plain(diag, [(v - CENTER) * (1.0 / HALF) + 3.0 * COEFF_ZERO * SCALE for v in new], j)
        return 0

    lax.fori_loop(0, 2 * BX, last_sweep, 0, unroll=6)

    def give(p, _):
        put_strips(pot, plain(fa, p + BX), turned(turn, p))
        return 0

    lax.fori_loop(0, BX, give, 0, unroll=2)
    save = pltpu.make_async_copy(pot, potential, sem.at[0])
    save.start()
    two_steps(sides, orb, far, near, diag, rest, y1, y2, zp, m)
    save.wait()


def first(sides, orb, core, far, near, mine, rho_far, rho_near, wts, fs, rest):
    f = jnp.float32
    return call(
        first_kernel,
        [(BX, NY, NZ), (2 * BX, *VEC), (NB, 2 * BX, *VEC), (NB, BX, *VEC)],
        [SM] + [VM] * 10,
        [HBM] + [VM] * 3,
        [
            pltpu.VMEM((3 * BX, *VEC), f),
            pltpu.VMEM((3 * BX, *VEC), f),
            pltpu.VMEM((3 * BX - 2, *VEC), f),
            pltpu.VMEM((2 * BX, *VEC), f),
            pltpu.VMEM((NB, BX, *VEC), f),
            pltpu.VMEM((BX, NY, NZ), f),
            pltpu.SemaphoreType.DMA((1,)),
        ],
        (sides, orb, core, far, near, mine, rho_far, rho_near, wts, fs, rest),
    )


def own_kernel(y1, y2, diag, turn_in, partial, zp):
    turn = turn_in[1]
    at = [turned(turn, p) for p in range(BX)]
    m = Masks()
    matrix = band_matrix()
    for o in range(NB):
        x = jnp.concatenate([y2[o, at[p]].reshape(NY, NZ) for p in range(BX)], axis=0)
        zp[o] = along_z(x, matrix).reshape(BX, *VEC)

    def step_three(o, _):
        for j in range(BX):
            part, mid = stencil(
                lambda dist: plain(y2, o, at[j + dist]) if 0 <= j + dist < BX else None, plain(zp, o, j), m, 2.0
            )
            old = plain(y1, o, j + 3)
            new = [2.0 * a * b + (c - d) for a, b, c, d in zip(plain(diag, j + 3), mid, part, old)]
            put_plain(partial, new, o, j)
        return 0

    lax.fori_loop(0, NB, step_three, 0)


def own(sides, y1, y2, diag):
    return call(
        own_kernel,
        [(NB, BX, *VEC)],
        [VM] * 3 + [SM],
        [VM],
        [pltpu.VMEM((NB, BX, *VEC), jnp.float32)],
        (y1, y2, diag, sides),
    )[0]


def last_kernel(sides, y1, y2, near, far, diag, partial, out, y3, zp, done, sems):
    has_far = sides[0] > 0
    turn = sides[1]
    at = [turned(turn, p) for p in range(BX)]
    m = Masks()
    matrix = band_matrix()
    for o in range(NB):
        for ref, planes, base in ((far, (3, 4, 5), 0), (near, (0, 1, 2), 3)):
            x = jnp.concatenate([ref[o, at[p]].reshape(NY, NZ) for p in planes], axis=0)
            zp[o, pl.ds(base, 3)] = along_z(x, matrix).reshape(3, *VEC)

    def step_three(o, _):
        def get(p):
            return plain((far, y2, near)[p // BX], o, at[p % BX])

        for j in (0, 1, 2, BX + 3, BX + 4, BX + 5):
            part, mid = stencil(lambda dist: get(j + 3 + dist), plain(zp, o, j if j < 3 else j - BX), m, 2.0)
            old = plain(y1, o, j)
            new = [2.0 * a * b + (c - d) for a, b, c, d in zip(plain(diag, j), mid, part, old)]
            if j < 3:
                new = [jnp.where(has_far, v, 0.0) for v in new]
            put_plain(y3, new, o, j)
        for j in range(BX):
            new = plain(partial, o, j)
            for dist, weight in zip((1, 2, 3), COEFFS):
                for p in (j - dist, j + dist):
                    if not 0 <= p < BX:
                        new = [a + (2.0 * SCALE * weight) * b for a, b in zip(new, get(p + BX))]
            put_plain(y3, new, o, j + 3)
        return 0

    lax.fori_loop(0, NB, step_three, 0)
    for o in range(NB):
        x = y3[o, pl.ds(3, BX)].reshape(BX * NY, NZ)
        zp[o] = along_z(x, matrix).reshape(BX, *VEC)

    def step_four(o, _):
        for j in range(BX):
            part, mid = stencil(lambda dist: plain(y3, o, j + 3 + dist), plain(zp, o, j), m, 2.0)
            old = plain(y2, o, at[j])
            new = [2.0 * a * b + (c - d) for a, b, c, d in zip(plain(diag, j + 3), mid, part, old)]
            put_strips(done, new, o, at[j])
        pltpu.make_async_copy(done.at[o], out.at[o], sems.at[o]).start()
        return 0

    lax.fori_loop(0, NB, step_four, 0)
    for o in range(NB):
        pltpu.make_async_copy(done.at[o], out.at[o], sems.at[o]).wait()


def last(sides, y1, y2, near, far, diag, partial):
    f = jnp.float32
    return call(
        last_kernel,
        [(NB, BX, NY, NZ)],
        [SM] + [VM] * 6,
        [HBM],
        [
            pltpu.VMEM((NB, 2 * BX, *VEC), f),
            pltpu.VMEM((NB, BX, *VEC), f),
            pltpu.VMEM((NB, BX, NY, NZ), f),
            pltpu.SemaphoreType.DMA((NB,)),
        ],
        (sides, y1, y2, near, far, diag, partial),
    )[0]


def swap_far(x):
    n = lax.axis_size("dom")
    return lax.ppermute(x, "dom", [p for i in range(1, n - 1, 2) for p in ((i, i + 1), (i + 1, i))])


def swap_near(x):
    n = lax.axis_size("dom")
    return lax.ppermute(x, "dom", [p for i in range(0, n - 1, 2) for p in ((i, i + 1), (i + 1, i))])


def local(orbitals, occupation, dielectric, core_density, start_field):
    bands = lax.axis_size("band")
    dom = lax.axis_index("dom")
    half = bands // 2
    groups = [list(range(half)), list(range(half, bands))]
    turn = dom % 2
    has_far = jnp.where(turn > 0, dom < lax.axis_size("dom") - 1, dom > 0)
    sides = jnp.stack([has_far.astype(jnp.int32), turn.astype(jnp.int32)])

    parts = density(half, occupation, orbitals)
    held, parts, sides = lax.optimization_barrier(
        ((orbitals, start_field, dielectric, core_density), parts, sides)
    )
    packed = pack(*held)
    parts = lax.all_to_all(parts, "band", 0, 0, axis_index_groups=groups)
    mine = jnp.sum(parts, axis=0)
    mine, packed = lax.optimization_barrier((mine, packed))
    other = lax.ppermute(mine, "band", [(i, (i + half) % bands) for i in range(bands)])
    far, near = swap_far(packed), swap_near(packed)
    got = lax.all_to_all(spread(half, mine, other), "band", 0, 0, axis_index_groups=groups)
    to_near, to_far = join(half, sides, got, far, near)
    rho_far, rho_near = swap_far(to_far), swap_near(to_near)
    (near, far), to_near = lax.optimization_barrier(((near, far), to_near))
    wts, fs, rest = prepare(sides, orbitals, dielectric, start_field, far, near)
    cells = (-1, NY, NZ)
    potential, diag, y1, y2 = first(
        sides, orbitals, core_density, far, near,
        to_near.reshape(cells), rho_far.reshape(cells), rho_near.reshape(cells), wts, fs, rest,
    )
    y2_far, y2_near = swap_far(y2), swap_near(y2)
    partial = own(sides, y1, y2, diag)
    return potential, last(sides, y1, y2, y2_near, y2_far, diag, partial)


def solution(mesh):
    return jax.shard_map(
        local,
        mesh=mesh,
        in_specs=(
            P("band", "dom", None, None),
            P("band"),
            P("dom", None, None),
            P("dom", None, None),
            P("dom", None, None),
        ),
        out_specs=(P("dom", None, None), P("band", "dom", None, None)),
        check_vma=False,
    )
```
